256 devices in a mesh: step: 32 (over z, x), seq: 8 (over y, core).
Axes of the slice: x: 4, y: 4, z: 8, core: 2. Of those that a mesh axis runs over, the one named last changes fastest.
Arguments:
- latents: bfloat16 [32, 8, 256, 1152], P('step', 'seq'), may hold values from -6 to 6
- timesteps: int32 [32], P('step'), may hold values from 0 to 31
- step_sizes: float32 [32], P('step'), may hold values from 0.02 to 0.15
- modulation: bfloat16 [32, 6912], replicated, may hold values from -4 to 4
- spatial_qkv: bfloat16 [1152, 1728], replicated, may hold values from -0.1875 to 0.1875
- spatial_out: bfloat16 [576, 1152], replicated, may hold values from -0.25 to 0.25
- temporal_qkv: bfloat16 [1152, 1728], replicated, may hold values from -0.1875 to 0.1875
- temporal_out: bfloat16 [576, 1152], replicated, may hold values from -0.25 to 0.25
Outputs:
- updated: bfloat16 [32, 8, 256, 1152], P('step', 'seq')
- change: float32 [32], P('step')
The draws below stay inside these ranges and needn't reach their ends.
All inputs are finite; a program needn't handle non-finite values.
Results may differ from the reference program's by a relative error of at most 0.01.
Values may be sent and summed in bfloat16 or wider, within the bound.
A program may use at most 128 MiB of HBM per device.

```python
import math
import jax
import jax.numpy as jnp
from jax import lax

D = 1152
HEADS = 8
HEAD_DIM = 72
PATCHES = 256
TABLE = 32
FRAMES = 8
STEPS = 32


def with_ends(values, key, low, high):
    spot = [jax.random.randint(jax.random.fold_in(key, axis), (), 0, length) for axis, length in enumerate(values.shape)]
    longest = values.shape.index(max(values.shape))
    next_to = spot[:longest] + [(spot[longest] + 1) % values.shape[longest]] + spot[longest + 1:]
    return values.at[tuple(spot)].set(low).at[tuple(next_to)].set(high)


def block_scale(own_key, extent, split, low, top_value):
    level = 1.0
    for axis_at, shards_of in split:
        steps = jax.random.uniform(jax.random.fold_in(jax.random.fold_in(own_key, 6), axis_at), (shards_of,), jnp.float32, low / len(split), top_value / len(split))
        level = level * jnp.repeat(jnp.exp(steps), extent[axis_at] // shards_of).reshape((-1,) + (1,) * (len(extent) - 1 - axis_at))
    return level


def gaussian(stream_key, dims, scale, reach, cuts=(), dtype=jnp.bfloat16):
    values = scale * jax.random.normal(stream_key, dims, jnp.float32)
    if cuts:
        values = values * block_scale(stream_key, dims, cuts, -0.22, 0.18)
    return jnp.clip(values, -reach, reach).astype(dtype)


def setup_inputs(seed: int = 0) -> dict:
    seeds = jax.random.split(jax.random.key(seed), 9)
    return {
        "latents": gaussian(seeds[0], (STEPS, FRAMES, PATCHES, D), 1.0, 6.0, ((0, 32), (1, 8))),
        "timesteps": with_ends(jax.random.randint(seeds[1], (STEPS,), 0, TABLE), jax.random.fold_in(seeds[1], 1), 0, TABLE - 1).astype(jnp.int32),
        "step_sizes": jnp.clip(jnp.exp(math.log(0.15) - 2.014903 * jax.random.uniform(seeds[2], (STEPS,), jnp.float32) ** block_scale(seeds[2], (STEPS,), ((0, 32),), -0.2, 0.2)), 0.02, 0.15),
        "modulation": gaussian(seeds[3], (TABLE, 6 * D), 0.8, 4.0),
        "spatial_qkv": gaussian(seeds[4], (D, 3 * HEADS * HEAD_DIM), D ** -0.5, 0.1875),
        "spatial_out": gaussian(seeds[5], (HEADS * HEAD_DIM, D), (HEADS * HEAD_DIM) ** -0.5, 0.25),
        "temporal_qkv": gaussian(seeds[6], (D, 3 * HEADS * HEAD_DIM), D ** -0.5, 0.1875),
        "temporal_out": gaussian(seeds[7], (HEADS * HEAD_DIM, D), (HEADS * HEAD_DIM) ** -0.5, 0.25),
    }


def layer_norm(values):
    values = values.astype(jnp.float32)
    center = values - lax.optimization_barrier(jnp.mean(values, axis=-1, keepdims=True))
    spread = lax.optimization_barrier(jnp.mean(center * center, axis=-1, keepdims=True))
    return center * lax.rsqrt(spread + 1e-06)

def unit_rows(values):
    return values * lax.rsqrt(lax.optimization_barrier(jnp.mean(values * values, axis=-1, keepdims=True)) + 1e-06)

def attend(inputs, w_project):
    batch, length = (inputs.shape[0], inputs.shape[1])
    projected = jnp.einsum('bld,de->ble', inputs.astype(jnp.float32), w_project.astype(jnp.float32))
    projected = projected.reshape(batch, length, 3, HEADS, HEAD_DIM)
    queries = unit_rows(projected[:, :, 0]).astype(jnp.bfloat16)
    keys = unit_rows(projected[:, :, 1]).astype(jnp.bfloat16)
    values = projected[:, :, 2].astype(jnp.bfloat16)
    scores = jnp.einsum('blhe,bmhe->bhlm', queries.astype(jnp.float32), keys.astype(jnp.float32))
    scores = scores * (3.0 / math.sqrt(HEAD_DIM))
    exponent = jnp.exp(scores)
    weights = (exponent / lax.optimization_barrier(jnp.sum(exponent, axis=-1, keepdims=True))).astype(jnp.bfloat16)
    mixed = jnp.einsum('bhlm,bmhe->blhe', weights.astype(jnp.float32), values.astype(jnp.float32))
    return mixed.astype(jnp.bfloat16).reshape(batch, length, HEADS * HEAD_DIM)

def project_out(heads_out, w_out):
    return jnp.einsum('ble,ed->bld', heads_out.astype(jnp.float32), w_out.astype(jnp.float32))

def drift(state, conditioning, spatial_qkv, spatial_out, temporal_qkv, temporal_out):
    spatial_in = (layer_norm(state) * (1.0 + conditioning[1]) + conditioning[0]).astype(jnp.bfloat16)
    spatial_heads = attend(spatial_in, spatial_qkv)
    after_spatial = (state.astype(jnp.float32) + conditioning[2] * project_out(spatial_heads, spatial_out)).astype(jnp.bfloat16)
    temporal_in = (layer_norm(after_spatial) * (1.0 + conditioning[4]) + conditioning[3]).astype(jnp.bfloat16)
    temporal_heads = jnp.swapaxes(attend(jnp.swapaxes(temporal_in, 0, 1), temporal_qkv), 0, 1)
    return after_spatial.astype(jnp.float32) + conditioning[5] * project_out(temporal_heads, temporal_out)

def reference(latents, timesteps, step_sizes, modulation, spatial_qkv, spatial_out, temporal_qkv, temporal_out):
    width = latents.shape[-1]
    conditions = modulation[timesteps].astype(jnp.float32).reshape(timesteps.shape[0], 6, width)

    def advance(running, inputs):
        state, conditioning, step_size = inputs
        drift_term = step_size * drift(state, conditioning, spatial_qkv, spatial_out, temporal_qkv, temporal_out)
        running = running + drift_term
        return (running, running.astype(jnp.bfloat16))
    start = latents[0].astype(jnp.float32)
    unused, updated = lax.scan(advance, start, (latents, conditions, step_sizes))
    following = jnp.concatenate([latents[1:], jnp.zeros_like(latents[:1])], axis=0)
    difference = updated.astype(jnp.float32) - following.astype(jnp.float32)
    change = lax.optimization_barrier(jnp.mean(difference * difference, axis=(1, 2, 3)))
    return (updated, change)
```

```python
import math

import jax
import jax.numpy as jnp
from jax import lax
from jax.experimental import pallas as pl
from jax.experimental.pallas import tpu as pltpu
from jax.sharding import PartitionSpec as P

MESH = pl.DeviceIdType.MESH
F32 = jnp.float32
BF16 = jnp.bfloat16

D = 1152
HEADS = 8
HEAD_DIM = 72
E = HEADS * HEAD_DIM
ROWS = 256
HALF = 128
PIECE = 16
NX = 4
NZ = 8
NS = 8
WIDE = 640
SHIFT = 512
EPS = 1e-6
LOG2E = 1.4426950408889634
Q_SCALE = 3.0 / math.sqrt(HEAD_DIM) * LOG2E


def layer_norm(values):
    center = values - jnp.mean(values, axis=-1, keepdims=True)
    spread = jnp.mean(center * center, axis=-1, keepdims=True)
    return center * lax.rsqrt(spread + EPS)


def project(inputs, w_ref, member, spread, qk, vals):
    raw = jnp.dot(inputs, w_ref[:, : 2 * E], preferred_element_type=F32)
    squares = jnp.dot((raw * raw).astype(BF16), member[...], preferred_element_type=F32)
    group = lax.broadcasted_iota(jnp.int32, squares.shape, 1)
    root = lax.rsqrt(squares * (1.0 / HEAD_DIM) + EPS)
    root = root * jnp.where(group < HEADS, Q_SCALE, 1.0)
    high = root.astype(BF16)
    low = (root - high.astype(F32)).astype(BF16)
    factor = jnp.dot(
        jnp.concatenate([high, low], axis=1), spread[...], preferred_element_type=F32
    )
    units = (raw * factor).astype(BF16)
    qk[0, :, :E] = units[:, :E]
    qk[1, :, :E] = units[:, E:]
    vals[:, :E] = jnp.dot(inputs, w_ref[:, 2 * E :], preferred_element_type=F32).astype(BF16)


def attend(qk, vals, rows, mask):
    count = rows.size
    ones = jnp.ones((count, 128), BF16)
    tiles = [None] * 5
    for head in range(HEADS):
        low, high = head * HEAD_DIM, (head + 1) * HEAD_DIM
        first, last = low // 128, (high - 1) // 128
        window = slice(first * 128, (last + 1) * 128)
        lane = lax.broadcasted_iota(jnp.int32, (count, window.stop - window.start), 1)
        lane = lane + window.start
        inside = jnp.logical_and(lane >= low, lane < high)
        queries = jnp.where(inside, qk[0, rows, window], jnp.zeros((), BF16))
        keys = jnp.where(inside, qk[1, rows, window], jnp.zeros((), BF16))
        scores = lax.dot_general(
            queries, keys, (((1,), (1,)), ((), ())), preferred_element_type=F32
        )
        weights = jnp.exp2(scores)
        if mask is not None:
            weights = jnp.where(mask, weights, 0.0)
        weights = weights.astype(BF16)
        total = jnp.dot(weights, ones, preferred_element_type=F32)
        inverse = 1.0 / total
        for t in range(first, last + 1):
            mixed = jnp.dot(
                weights, vals[rows, t * 128 : (t + 1) * 128], preferred_element_type=F32
            )
            mixed = mixed * inverse
            if tiles[t] is None:
                tiles[t] = mixed
            else:
                at = lax.broadcasted_iota(jnp.int32, mixed.shape, 1) + t * 128
                tiles[t] = jnp.where(at >= low, mixed, tiles[t])
    return tiles


def kernel(
    lat_hbm, time_ref, size_ref, mod_hbm, w1_hbm, o1_hbm, w2_hbm, o2_hbm,
    out_hbm, change_ref,
    lat, mod, w1, o1, w2, o2, member, spread, qk, vals, heads, cond,
    following, after, anchor, mine, drift, x_in, total, z_in, carry, c_in, done, u_in, out,
    part, parts,
    local_sem, next_send, next_recv, anchor_send, anchor_recv, y_send, y_recv,
    x_send, x_recv, z_send, z_recv, c_send, c_recv, u_send, u_recv, p_send, p_recv, out_sem,
):
    me = lax.axis_index("step")
    s = lax.axis_index("seq")
    z, x = me // NX, lax.rem(me, NX)
    rp, cg = x // 2, lax.rem(x, 2)

    loads = [
        pltpu.make_async_copy(src, dst, local_sem.at[i])
        for i, (src, dst) in enumerate(
            [(lat_hbm, lat), (mod_hbm, mod), (w1_hbm, w1), (o1_hbm, o1), (w2_hbm, w2), (o2_hbm, o2)]
        )
    ]
    for load in loads:
        load.start()

    def to(step, seq):
        return {"step": step, "seq": seq}

    barrier = pltpu.get_barrier_semaphore()
    before = lax.rem(me + NX * NZ - 1, NX * NZ)
    behind = lax.rem(me + 1, NX * NZ)

    def greet_plane(k, _):
        other_s = lax.rem(s + lax.rem(k, NS), NS)
        other_x = lax.rem(x + k // NS, NX)
        pl.semaphore_signal(barrier, inc=1, device_id=to(z * NX + other_x, other_s), device_id_type=MESH)
        return _

    lax.fori_loop(1, NX * NS, greet_plane, 0)

    def greet_planes(k, _):
        other_z = lax.rem(z + k, NZ)
        pl.semaphore_signal(barrier, inc=1, device_id=to(other_z * NX + x, s), device_id_type=MESH)
        return _

    lax.fori_loop(1, NZ, greet_planes, 0)
    for step in (before, behind):
        pl.semaphore_signal(barrier, inc=1, device_id=to(step, s), device_id_type=MESH)

    column = lax.broadcasted_iota(jnp.int32, (2 * E, 128), 0)
    head = lax.broadcasted_iota(jnp.int32, (2 * E, 128), 1) * HEAD_DIM
    member[...] = jnp.where(
        jnp.logical_and(column >= head, column < head + HEAD_DIM), 1.0, 0.0
    ).astype(BF16)
    column = lax.broadcasted_iota(jnp.int32, (256, 2 * E), 1)
    head = lax.rem(lax.broadcasted_iota(jnp.int32, (256, 2 * E), 0), 128) * HEAD_DIM
    spread[...] = jnp.where(
        jnp.logical_and(column >= head, column < head + HEAD_DIM), 1.0, 0.0
    ).astype(BF16)

    loads[1].wait()
    one_hot = (lax.broadcasted_iota(jnp.int32, (16, mod.shape[0]), 1) == time_ref[0]).astype(BF16)
    cond[...] = jnp.dot(one_hot, mod[...], preferred_element_type=F32)

    def vector(i):
        return cond[0:1, i * D : (i + 1) * D]

    loads[0].wait()
    spatial_in = (layer_norm(lat[...].astype(F32)) * (1.0 + vector(1)) + vector(0)).astype(BF16)

    pl.semaphore_wait(barrier, NX * NS - 1 + NZ - 1 + 2)
    send_next = pltpu.make_async_remote_copy(
        src_ref=lat, dst_ref=following, send_sem=next_send, recv_sem=next_recv,
        device_id=to(before, s), device_id_type=MESH,
    )
    send_next.start()

    def piece(k, half):
        return pl.ds(pl.multiple_of(half * HALF + k * PIECE, PIECE), PIECE)

    def y_copy(src, dst, send, recv, k, half, sender, target):
        return pltpu.make_async_remote_copy(
            src_ref=src.at[piece(target, half), :], dst_ref=dst.at[piece(sender, half), :],
            send_sem=send.at[half, k], recv_sem=recv.at[half, sender],
            device_id=to(me, target), device_id_type=MESH,
        )

    def y_start(src, dst, send, recv):
        def start(k, _):
            for half in range(2):
                y_copy(src, dst, send, recv, k, half, s, lax.rem(s + k, NS)).start()
            return _

        lax.fori_loop(1, NS, start, 0)

    def y_wait(src, dst, send, recv, arrived):
        def wait(k, _):
            for half in range(2):
                copy = y_copy(src, dst, send, recv, k, half, lax.rem(s + k, NS), s)
                if arrived:
                    copy.wait_recv()
                else:
                    copy.wait_send()
            return _

        lax.fori_loop(1, NS, wait, 0)

    def keep_own(src, dst):
        for half in range(2):
            dst[piece(s, half), :] = src[piece(s, half), :]

    @pl.when(me == 0)
    def _():
        y_start(lat, anchor, anchor_send, anchor_recv)
        keep_own(lat, anchor)

    def put_heads(rows, tiles):
        for t in range(4):
            heads[rows, t * 128 : (t + 1) * 128] = tiles[t].astype(BF16)
        heads[rows, 512:E] = tiles[4][:, : E - 512].astype(BF16)

    loads[2].wait()
    project(spatial_in, w1, member, spread, qk, vals)
    everything = pl.ds(0, ROWS)
    put_heads(everything, attend(qk, vals, everything, None))
    loads[3].wait()
    after[...] = (
        lat[...].astype(F32) + vector(2) * jnp.dot(heads[...], o1[...], preferred_element_type=F32)
    ).astype(BF16)

    y_start(after, mine, y_send, y_recv)
    keep_own(after, mine)
    loads[4].wait()
    loads[5].wait()
    y_wait(after, mine, y_send, y_recv, True)

    own = mine[...].astype(F32)
    temporal_in = (layer_norm(own) * (1.0 + vector(4)) + vector(3)).astype(BF16)
    project(temporal_in, w2, member, spread, qk, vals)
    patch = lax.rem(lax.broadcasted_iota(jnp.int32, (HALF, HALF), 0), PIECE)
    patch_of_key = lax.rem(lax.broadcasted_iota(jnp.int32, (HALF, HALF), 1), PIECE)
    for half in range(2):
        rows = pl.ds(half * HALF, HALF)
        put_heads(rows, attend(qk, vals, rows, patch == patch_of_key))
    term = size_ref[0] * (
        mine[...].astype(F32) + vector(5) * jnp.dot(heads[...], o2[...], preferred_element_type=F32)
    )
    drift[...] = term.astype(BF16)

    @pl.when(me == 0)
    def _():
        y_wait(lat, anchor, anchor_send, anchor_recv, True)
        drift[...] = (drift[...].astype(F32) + anchor[...].astype(F32)).astype(BF16)

    def block(holder):
        row = pl.multiple_of((holder // 2) * HALF, HALF)
        col = pl.multiple_of(lax.rem(holder, 2) * SHIFT, 128)
        return pl.ds(row, HALF), pl.ds(col, WIDE)

    def x_copy(k, sender, target):
        rows, cols = block(target)
        return pltpu.make_async_remote_copy(
            src_ref=drift.at[rows, cols], dst_ref=x_in.at[sender],
            send_sem=x_send.at[k], recv_sem=x_recv.at[sender],
            device_id=to(z * NX + target, s), device_id_type=MESH,
        )

    for k in range(1, NX):
        x_copy(k, x, lax.rem(x + k, NX)).start()
    rows, cols = block(x)
    x_in[x] = drift[rows, cols]
    for k in range(1, NX):
        x_copy(k, lax.rem(x + k, NX), x).wait_recv()
    total[...] = (
        x_in[0].astype(F32) + x_in[1].astype(F32) + x_in[2].astype(F32) + x_in[3].astype(F32)
    ).astype(BF16).reshape(NZ, PIECE, WIDE)

    def z_copy(k, sender, target):
        return pltpu.make_async_remote_copy(
            src_ref=total.at[target], dst_ref=z_in.at[sender],
            send_sem=z_send.at[k], recv_sem=z_recv.at[sender],
            device_id=to(target * NX + x, s), device_id_type=MESH,
        )

    def c_copy(k, sender, target):
        return pltpu.make_async_remote_copy(
            src_ref=carry.at[target], dst_ref=c_in.at[sender],
            send_sem=c_send.at[k], recv_sem=c_recv.at[sender],
            device_id=to(target * NX + x, s), device_id_type=MESH,
        )

    for k in range(1, NZ):
        z_copy(k, z, lax.rem(z + k, NZ)).start()
    z_in[z] = total[z]
    for k in range(1, NZ):
        z_copy(k, lax.rem(z + k, NZ), z).wait_recv()
    running = jnp.zeros((PIECE, WIDE), F32)
    for k in range(NZ):
        carry[k] = running.astype(BF16)
        running = running + z_in[k].astype(F32)
    for k in range(1, NZ):
        c_copy(k, z, lax.rem(z + k, NZ)).start()
    c_in[z] = carry[z]
    for k in range(1, NZ):
        c_copy(k, lax.rem(z + k, NZ), z).wait_recv()

    running = c_in[...].astype(F32).reshape(HALF, WIDE)
    for k in range(NX):
        running = running + x_in[k].astype(F32)
        done[k] = running.astype(BF16).reshape(NS, PIECE, WIDE)

    def u_copy(k, x_from, s_from, x_to, s_to):
        row = pl.multiple_of((x_from // 2) * HALF + s_from * PIECE, PIECE)
        return pltpu.make_async_remote_copy(
            src_ref=done.at[x_to, s_to],
            dst_ref=u_in.at[lax.rem(x_from, 2), pl.ds(row, PIECE), :],
            send_sem=u_send.at[k], recv_sem=u_recv.at[x_from, s_from],
            device_id=to(z * NX + x_to, s_to), device_id_type=MESH,
        )

    def u_start(k, _):
        u_copy(k, x, s, lax.rem(x + k // NS, NX), lax.rem(s + lax.rem(k, NS), NS)).start()
        return _

    def u_wait(k, _):
        u_copy(k, lax.rem(x + k // NS, NX), lax.rem(s + lax.rem(k, NS), NS), x, s).wait_recv()
        return _

    lax.fori_loop(1, NX * NS, u_start, 0)
    u_in[cg, piece(s, rp), :] = done[x, s]
    send_next.wait_recv()
    lax.fori_loop(1, NX * NS, u_wait, 0)

    out[:, :WIDE] = u_in[0]
    out[:, WIDE:] = u_in[1, :, 128:]
    store = pltpu.make_async_copy(out, out_hbm, out_sem)
    store.start()
    known = jnp.where(me == NX * NZ - 1, 0.0, 1.0)
    after_this = jnp.where(known > 0.5, following[...].astype(F32), 0.0)
    difference = out[...].astype(F32) - after_this
    squares = (difference * difference).reshape(ROWS // 8, 8, D).sum(axis=0)
    tile = squares[:, :128]
    for t in range(1, D // 128):
        tile = tile + squares[:, t * 128 : (t + 1) * 128]
    part[...] = tile

    def p_copy(k, sender, target):
        return pltpu.make_async_remote_copy(
            src_ref=part, dst_ref=parts.at[sender],
            send_sem=p_send.at[k], recv_sem=p_recv.at[sender],
            device_id=to(me, target), device_id_type=MESH,
        )

    for k in range(1, NS):
        p_copy(k, s, lax.rem(s + k, NS)).start()
    parts[s] = part[...]
    for k in range(1, NS):
        p_copy(k, lax.rem(s + k, NS), s).wait_recv()
    change_ref[0] = jnp.sum(jnp.sum(parts[...], axis=0)) * (1.0 / (NS * ROWS * D))

    send_next.wait_send()

    @pl.when(me == 0)
    def _():
        y_wait(lat, anchor, anchor_send, anchor_recv, False)

    y_wait(after, mine, y_send, y_recv, False)
    for k in range(1, NX):
        x_copy(k, x, lax.rem(x + k, NX)).wait_send()
    for k in range(1, NZ):
        z_copy(k, z, lax.rem(z + k, NZ)).wait_send()
        c_copy(k, z, lax.rem(z + k, NZ)).wait_send()

    def u_left(k, _):
        u_copy(k, x, s, lax.rem(x + k // NS, NX), lax.rem(s + lax.rem(k, NS), NS)).wait_send()
        return _

    lax.fori_loop(1, NX * NS, u_left, 0)
    for k in range(1, NS):
        p_copy(k, s, lax.rem(s + k, NS)).wait_send()
    store.wait()


def body(latents, timesteps, step_sizes, modulation, spatial_qkv, spatial_out, temporal_qkv, temporal_out):
    dma = pltpu.SemaphoreType.DMA
    anywhere = pl.BlockSpec(memory_space=pl.ANY)
    scalar = pl.BlockSpec(memory_space=pltpu.SMEM)

    def vmem(*shape, dtype=BF16):
        return pltpu.VMEM(shape, dtype)

    table = modulation.shape[0]
    updated, change = pl.pallas_call(
        kernel,
        out_shape=(jax.ShapeDtypeStruct((ROWS, D), BF16), jax.ShapeDtypeStruct((1,), F32)),
        in_specs=[anywhere, scalar, scalar] + [anywhere] * 5,
        out_specs=(anywhere, scalar),
        scratch_shapes=[
            vmem(ROWS, D), vmem(table, 6 * D),
            vmem(D, 3 * E), vmem(E, D), vmem(D, 3 * E), vmem(E, D),
            vmem(2 * E, 128), vmem(256, 2 * E),
            vmem(2, ROWS, 640), vmem(ROWS, 640), vmem(ROWS, E), vmem(16, 6 * D, dtype=F32),
            vmem(ROWS, D), vmem(ROWS, D), vmem(ROWS, D), vmem(ROWS, D), vmem(ROWS, D),
            vmem(NX, HALF, WIDE), vmem(NZ, PIECE, WIDE), vmem(NZ, PIECE, WIDE),
            vmem(NZ, PIECE, WIDE), vmem(NZ, PIECE, WIDE),
            vmem(NX, NS, PIECE, WIDE), vmem(2, ROWS, WIDE), vmem(ROWS, D),
            vmem(8, 128, dtype=F32), vmem(NS, 8, 128, dtype=F32),
            dma((6,)), dma, dma, dma((2, NS)), dma((2, NS)), dma((2, NS)), dma((2, NS)),
            dma((NX,)), dma((NX,)), dma((NZ,)), dma((NZ,)), dma((NZ,)), dma((NZ,)),
            dma((NX * NS,)), dma((NX, NS)), dma((NS,)), dma((NS,)), dma,
        ],
        compiler_params=pltpu.CompilerParams(
            collective_id=0, has_side_effects=True, vmem_limit_bytes=48 * 1024 * 1024
        ),
        cost_estimate=pl.CostEstimate(
            flops=2800000000, bytes_accessed=12000000, transcendentals=1000000
        ),
    )(
        latents.reshape(ROWS, D), timesteps, step_sizes, modulation,
        spatial_qkv, spatial_out, temporal_qkv, temporal_out,
    )
    return updated[None, None], change


def solution(mesh):
    in_specs = (P("step", "seq", None, None), P("step"), P("step"), P(), P(), P(), P(), P())
    out_specs = (P("step", "seq", None, None), P("step"))
    return jax.shard_map(body, mesh=mesh, in_specs=in_specs, out_specs=out_specs, check_vma=False)
```

```python
import math

import jax
import jax.numpy as jnp
from jax import lax
from jax.experimental import pallas as pl
from jax.experimental.pallas import tpu as pltpu
from jax.sharding import PartitionSpec as P

UNROLL = 8
MESH = pl.DeviceIdType.MESH
F32 = jnp.float32
BF16 = jnp.bfloat16

D = 1152
HEADS = 8
HEAD_DIM = 72
E = HEADS * HEAD_DIM
ROWS = 256
HALF = 128
PIECE = 16
NX = 4
NZ = 8
NS = 8
QUART = 64
WIDE = 640
SHIFT = 512
EPS = 1e-6
LOG2E = 1.4426950408889634
Q_SCALE = 3.0 / math.sqrt(HEAD_DIM) * LOG2E


def layer_norm(values):
    center = values - jnp.mean(values, axis=-1, keepdims=True)
    spread = jnp.mean(center * center, axis=-1, keepdims=True)
    return center * lax.rsqrt(spread + EPS)


def attend(raw, heads, queries, mask):
    def unit(rows, columns, scale):
        values = raw[rows, columns]
        squares = jnp.sum(values * values, axis=0, keepdims=True)
        return (values * (lax.rsqrt(squares * (1.0 / HEAD_DIM) + EPS) * scale)).astype(BF16)

    def one_head(head, _):
        first = [pl.multiple_of(i * E + head * HEAD_DIM, 8) for i in range(3)]
        asked = unit(pl.ds(first[0], HEAD_DIM), queries, Q_SCALE)
        keys = unit(pl.ds(first[1], HEAD_DIM), slice(None), 1.0)
        scores = lax.dot_general(keys, asked, (((0,), (0,)), ((), ())), preferred_element_type=F32)
        weights = jnp.exp2(scores)
        if mask is not None:
            weights = jnp.where(mask, weights, 0.0)
        inverse = 1.0 / jnp.sum(weights, axis=0, keepdims=True)
        values = raw[pl.ds(first[2], HEAD_DIM), :].astype(BF16)
        mixed = jnp.dot(values, weights.astype(BF16), preferred_element_type=F32)
        heads[pl.ds(first[0], HEAD_DIM), :] = mixed * inverse
        return _

    lax.fori_loop(0, HEADS, one_head, 0, unroll=UNROLL)


def kernel(
    lat_hbm, time_ref, size_ref, mod_hbm, w1_hbm, o1_hbm, w2_hbm, o2_hbm,
    out_hbm, change_ref,
    lat, mod, w1, o1, w2, o2, cond, inputs, raw, raw_half, heads,
    following, after, anchor, mine, drift, x_in, total, z_in, carry, c_in, done, u_in, out,
    part, parts,
    local_sem, next_send, next_recv, anchor_send, anchor_recv, y_send, y_recv,
    x_send, x_recv, z_send, z_recv, c_send, c_recv, u_send, u_recv, p_send, p_recv, out_sem,
):
    me = lax.axis_index("step")
    s = lax.axis_index("seq")
    z, x = me // NX, lax.rem(me, NX)
    fh, cg = x // 2, lax.rem(x, 2)

    loads = [
        pltpu.make_async_copy(src, dst, local_sem.at[i])
        for i, (src, dst) in enumerate(
            [(lat_hbm, lat), (mod_hbm, mod), (w1_hbm, w1), (o1_hbm, o1), (w2_hbm, w2), (o2_hbm, o2)]
        )
    ]
    for load in loads:
        load.start()

    def to(step, seq):
        return {"step": step, "seq": seq}

    barrier = pltpu.get_barrier_semaphore()
    before = lax.rem(me + NX * NZ - 1, NX * NZ)
    behind = lax.rem(me + 1, NX * NZ)

    def greet_plane(k, _):
        other_s = lax.rem(s + lax.rem(k, NS), NS)
        other_x = lax.rem(x + k // NS, NX)
        pl.semaphore_signal(barrier, inc=1, device_id=to(z * NX + other_x, other_s), device_id_type=MESH)
        return _

    lax.fori_loop(1, NX * NS, greet_plane, 0)

    def greet_planes(k, _):
        other_z = lax.rem(z + k, NZ)
        pl.semaphore_signal(barrier, inc=1, device_id=to(other_z * NX + x, s), device_id_type=MESH)
        return _

    lax.fori_loop(1, NZ, greet_planes, 0)
    for step in (before, behind):
        pl.semaphore_signal(barrier, inc=1, device_id=to(step, s), device_id_type=MESH)

    loads[1].wait()
    one_hot = (lax.broadcasted_iota(jnp.int32, (16, mod.shape[0]), 1) == time_ref[0]).astype(BF16)
    cond[...] = jnp.dot(one_hot, mod[...], preferred_element_type=F32)[:8]

    def vector(i):
        return cond[0:1, i * D : (i + 1) * D]

    def condition(src, start, count, shift, scale):
        def some(i, _):
            rows = pl.ds(pl.multiple_of(start + i * PIECE, PIECE), PIECE)
            normal = layer_norm(src[rows, :].astype(F32))
            inputs[rows, :] = (normal * (1.0 + vector(scale)) + vector(shift)).astype(BF16)
            return _

        lax.fori_loop(0, count // PIECE, some, 0, unroll=2)

    def piece(k, half):
        return pl.ds(pl.multiple_of(half * HALF + k * PIECE, PIECE), PIECE)

    def y_copy(src, dst, send, recv, k, half, sender, target):
        return pltpu.make_async_remote_copy(
            src_ref=src.at[piece(target, half), :], dst_ref=dst.at[piece(sender, half), :],
            send_sem=send.at[half, k], recv_sem=recv.at[half, sender],
            device_id=to(me, target), device_id_type=MESH,
        )

    def y_start(src, dst, send, recv, half):
        def start(k, _):
            y_copy(src, dst, send, recv, k, half, s, lax.rem(s + k, NS)).start()
            return _

        lax.fori_loop(1, NS, start, 0)
        dst[piece(s, half), :] = src[piece(s, half), :]

    def y_wait(src, dst, send, recv, half, arrived):
        def wait(k, _):
            copy = y_copy(src, dst, send, recv, k, half, lax.rem(s + k, NS), s)
            if arrived:
                copy.wait_recv()
            else:
                copy.wait_send()
            return _

        lax.fori_loop(1, NS, wait, 0)

    loads[0].wait()
    condition(lat, 0, ROWS, 0, 1)
    pl.semaphore_wait(barrier, NX * NS - 1 + NZ - 1 + 2)

    @pl.when(me == 0)
    def _():
        for half in range(2):
            y_start(lat, anchor, anchor_send, anchor_recv, half)

    send_next = pltpu.make_async_remote_copy(
        src_ref=lat, dst_ref=following, send_sem=next_send, recv_sem=next_recv,
        device_id=to(before, s), device_id_type=MESH,
    )
    send_next.start()

    contract_last = (((1,), (1,)), ((), ()))
    contract_first = (((0,), (0,)), ((), ()))
    halves = [slice(half * HALF, (half + 1) * HALF) for half in range(2)]

    loads[2].wait()
    raw[...] = lax.dot_general(w1[...], inputs[...], contract_last, preferred_element_type=F32)
    for half in range(2):
        rows = halves[half]
        attend(raw, heads, rows, None)
        if half == 0:
            loads[3].wait()
        shown = lax.dot_general(heads[...].astype(BF16), o1[...], contract_first, preferred_element_type=F32)
        after[rows, :] = (lat[rows, :].astype(F32) + vector(2) * shown).astype(BF16)
        y_start(after, mine, y_send, y_recv, half)
    loads[4].wait()
    loads[5].wait()

    def block(half, holder):
        row = pl.multiple_of(half * HALF + (holder // 2) * QUART, QUART)
        col = pl.multiple_of(lax.rem(holder, 2) * SHIFT, 128)
        return pl.ds(row, QUART), pl.ds(col, WIDE)

    def x_copy(half, k, sender, target):
        rows, cols = block(half, target)
        return pltpu.make_async_remote_copy(
            src_ref=drift.at[rows, cols], dst_ref=x_in.at[half, sender],
            send_sem=x_send.at[half, k], recv_sem=x_recv.at[half, sender],
            device_id=to(z * NX + target, s), device_id_type=MESH,
        )

    patch = lax.rem(lax.broadcasted_iota(jnp.int32, (HALF, HALF), 0), PIECE)
    patch_of_key = lax.rem(lax.broadcasted_iota(jnp.int32, (HALF, HALF), 1), PIECE)
    for half in range(2):
        rows = halves[half]
        y_wait(after, mine, y_send, y_recv, half, True)
        condition(mine, half * HALF, HALF, 3, 4)
        raw_half[...] = lax.dot_general(w2[...], inputs[rows, :], contract_last, preferred_element_type=F32)
        attend(raw_half, heads, slice(None), patch == patch_of_key)
        shown = lax.dot_general(heads[...].astype(BF16), o2[...], contract_first, preferred_element_type=F32)
        drift[rows, :] = (size_ref[0] * (mine[rows, :].astype(F32) + vector(5) * shown)).astype(BF16)

        @pl.when(me == 0)
        def _():
            y_wait(lat, anchor, anchor_send, anchor_recv, half, True)
            drift[rows, :] = (drift[rows, :].astype(F32) + anchor[rows, :].astype(F32)).astype(BF16)

        for k in range(1, NX):
            x_copy(half, k, x, lax.rem(x + k, NX)).start()
        own_rows, own_cols = block(half, x)
        x_in[half, x] = drift[own_rows, own_cols]

    def z_copy(half, frame, sender, target):
        return pltpu.make_async_remote_copy(
            src_ref=total.at[half, frame], dst_ref=z_in.at[sender],
            send_sem=z_send.at[half, frame], recv_sem=z_recv.at[sender],
            device_id=to(target * NX + x, s), device_id_type=MESH,
        )

    for half in range(2):
        for k in range(1, NX):
            x_copy(half, k, lax.rem(x + k, NX), x).wait_recv()
        block_sum = x_in[half, 0].astype(F32)
        for k in range(1, NX):
            block_sum = block_sum + x_in[half, k].astype(F32)
        total[half] = block_sum.astype(BF16).reshape(NX, PIECE, WIDE)
        for frame in range(4):
            target = 2 * frame + half

            @pl.when(z != target)
            def _():
                z_copy(half, frame, z, target).start()

            @pl.when(z == target)
            def _():
                z_in[z] = total[half, frame]

    def c_copy(half, k, holder, target):
        return pltpu.make_async_remote_copy(
            src_ref=carry.at[target], dst_ref=c_in.at[half, holder // 2],
            send_sem=c_send.at[k], recv_sem=c_recv.at[half, holder // 2],
            device_id=to(target * NX + x, s), device_id_type=MESH,
        )

    for half in range(2):

        @pl.when(lax.rem(z, 2) == half)
        def _():
            for k in range(1, NZ):
                z_copy(half, 0, lax.rem(z + k, NZ), z).wait_recv()
            running = jnp.zeros((PIECE, WIDE), F32)
            for k in range(NZ):
                carry[k] = running.astype(BF16)
                running = running + z_in[k].astype(F32)
            for k in range(1, NZ):
                c_copy(half, k, z, lax.rem(z + k, NZ)).start()
            c_in[half, z // 2] = carry[z]

    def u_copy(half, k, x_from, s_from, x_to, frame):
        return pltpu.make_async_remote_copy(
            src_ref=done.at[half, x_to, frame],
            dst_ref=u_in.at[lax.rem(x_from, 2), piece(s_from, half), :],
            send_sem=u_send.at[half, k], recv_sem=u_recv.at[half, lax.rem(x_from, 2), s_from],
            device_id=to(z * NX + x_to, (x_from // 2) * 4 + frame), device_id_type=MESH,
        )

    def u_each(half, do):
        def step(k, held):
            x_to, frame = lax.rem(x + k // 4, NX), lax.rem(k, 4)
            copy = u_copy(half, k, x, s, x_to, frame)

            @pl.when(jnp.logical_or(x_to != x, fh * 4 + frame != s))
            def _():
                do(copy)

            return held

        lax.fori_loop(0, NX * 4, step, 0)

    for half in range(2):
        for frame in range(4):

            @pl.when(z != 2 * frame + half)
            def _():
                c_copy(half, 0, 2 * frame + half, z).wait_recv()

        running = c_in[half].astype(F32).reshape(QUART, WIDE)
        for k in range(NX):
            running = running + x_in[half, k].astype(F32)
            done[half, k] = running.astype(BF16).reshape(4, PIECE, WIDE)
        u_each(half, lambda copy: copy.start())

        @pl.when(s // 4 == fh)
        def _():
            u_in[cg, piece(s, half), :] = done[half, x, lax.rem(s, 4)]

    send_next.wait_recv()
    known = jnp.where(me == NX * NZ - 1, 0.0, 1.0)
    part[...] = jnp.zeros_like(part)
    stores = []
    for half in range(2):
        rows = halves[half]

        def arrive(k, held):
            group, sender = k // NS, lax.rem(k, NS)
            x_from = (s // 4) * 2 + group

            @pl.when(jnp.logical_or(x_from != x, sender != s))
            def _():
                u_copy(half, 0, x_from, sender, x, lax.rem(s, 4)).wait_recv()

            return held

        lax.fori_loop(0, 2 * NS, arrive, 0)
        out[rows, :WIDE] = u_in[0, rows, :]
        out[rows, WIDE:] = u_in[1, rows, 128:]
        store = pltpu.make_async_copy(out.at[rows, :], out_hbm.at[rows, :], out_sem.at[half])
        store.start()
        stores.append(store)
        goal = jnp.where(known > 0.5, following[rows, :].astype(F32), 0.0)
        difference = out[rows, :].astype(F32) - goal
        squares = (difference * difference).reshape(HALF // 8, 8, D).sum(axis=0)
        for t in range(D // 128):
            part[...] += squares[:, t * 128 : (t + 1) * 128]

    def p_copy(k, sender, target):
        return pltpu.make_async_remote_copy(
            src_ref=part, dst_ref=parts.at[sender],
            send_sem=p_send.at[k], recv_sem=p_recv.at[sender],
            device_id=to(me, target), device_id_type=MESH,
        )

    for k in range(1, NS):
        p_copy(k, s, lax.rem(s + k, NS)).start()
    parts[s] = part[...]
    for k in range(1, NS):
        p_copy(k, lax.rem(s + k, NS), s).wait_recv()
    change_ref[0] = jnp.sum(jnp.sum(parts[...], axis=0)) * (1.0 / (NS * ROWS * D))

    send_next.wait_send()
    for half in range(2):

        @pl.when(me == 0)
        def _():
            y_wait(lat, anchor, anchor_send, anchor_recv, half, False)

        y_wait(after, mine, y_send, y_recv, half, False)
        for k in range(1, NX):
            x_copy(half, k, x, lax.rem(x + k, NX)).wait_send()
        for frame in range(4):

            @pl.when(z != 2 * frame + half)
            def _():
                z_copy(half, frame, z, 2 * frame + half).wait_send()

        u_each(half, lambda copy: copy.wait_send())
    for k in range(1, NZ):
        c_copy(0, k, z, lax.rem(z + k, NZ)).wait_send()
    for k in range(1, NS):
        p_copy(k, s, lax.rem(s + k, NS)).wait_send()
    for store in stores:
        store.wait()


def body(latents, timesteps, step_sizes, modulation, spatial_qkv, spatial_out, temporal_qkv, temporal_out):
    dma = pltpu.SemaphoreType.DMA
    anywhere = pl.BlockSpec(memory_space=pl.ANY)
    scalar = pl.BlockSpec(memory_space=pltpu.SMEM)

    def vmem(*shape, dtype=BF16):
        return pltpu.VMEM(shape, dtype)

    table = modulation.shape[0]
    updated, change = pl.pallas_call(
        kernel,
        out_shape=(jax.ShapeDtypeStruct((ROWS, D), BF16), jax.ShapeDtypeStruct((1,), F32)),
        in_specs=[anywhere, scalar, scalar] + [anywhere] * 5,
        out_specs=(anywhere, scalar),
        scratch_shapes=[
            vmem(ROWS, D), vmem(table, 6 * D),
            vmem(3 * E, D), vmem(E, D), vmem(3 * E, D), vmem(E, D),
            vmem(8, 6 * D, dtype=F32), vmem(ROWS, D),
            vmem(3 * E, ROWS, dtype=F32), vmem(3 * E, HALF, dtype=F32), vmem(E, HALF, dtype=F32),
            vmem(ROWS, D), vmem(ROWS, D), vmem(ROWS, D), vmem(ROWS, D), vmem(ROWS, D),
            vmem(2, NX, QUART, WIDE), vmem(2, 4, PIECE, WIDE), vmem(NZ, PIECE, WIDE),
            vmem(NZ, PIECE, WIDE), vmem(2, 4, PIECE, WIDE),
            vmem(2, NX, 4, PIECE, WIDE), vmem(2, ROWS, WIDE), vmem(ROWS, D),
            vmem(8, 128, dtype=F32), vmem(NS, 8, 128, dtype=F32),
            dma((6,)), dma, dma, dma((2, NS)), dma((2, NS)), dma((2, NS)), dma((2, NS)),
            dma((2, NX)), dma((2, NX)), dma((2, 4)), dma((NZ,)), dma((NZ,)), dma((2, 4)),
            dma((2, NX * 4)), dma((2, 2, NS)), dma((NS,)), dma((NS,)), dma((2,)),
        ],
        compiler_params=pltpu.CompilerParams(
            collective_id=0, has_side_effects=True, vmem_limit_bytes=56 * 1024 * 1024
        ),
        cost_estimate=pl.CostEstimate(
            flops=2800000000, bytes_accessed=12000000, transcendentals=1000000
        ),
    )(
        latents.reshape(ROWS, D), timesteps, step_sizes, modulation,
        spatial_qkv.T, spatial_out, temporal_qkv.T, temporal_out,
    )
    return updated[None, None], change


def solution(mesh):
    in_specs = (P("step", "seq", None, None), P("step"), P("step"), P(), P(), P(), P(), P())
    out_specs = (P("step", "seq", None, None), P("step"))
    return jax.shard_map(body, mesh=mesh, in_specs=in_specs, out_specs=out_specs, check_vma=False)
```

```python
import math

import jax
import jax.numpy as jnp
from jax import lax
from jax.experimental import pallas as pl
from jax.experimental.pallas import tpu as pltpu
from jax.sharding import PartitionSpec as P

UNROLL = 7
NORM_ROWS = 128
PROJECT = 1728
MESH = pl.DeviceIdType.MESH
F32 = jnp.float32
BF16 = jnp.bfloat16

D = 1152
HEADS = 8
HEAD_DIM = 72
E = HEADS * HEAD_DIM
ROWS = 256
HALF = 128
PIECE = 16
NX = 4
NZ = 8
NS = 8
QUART = 64
WIDE = 640
SHIFT = 512
EPS = 1e-6
LOG2E = 1.4426950408889634
Q_SCALE = 3.0 / math.sqrt(HEAD_DIM) * LOG2E


def layer_norm(values):
    center = values - jnp.mean(values, axis=-1, keepdims=True)
    spread = jnp.mean(center * center, axis=-1, keepdims=True)
    return center * lax.rsqrt(spread + EPS)


def attend(raw, heads, scores, blocks, mask):
    def unit(start, scale):
        values = raw[pl.ds(pl.multiple_of(start, 8), HEAD_DIM), :]
        squares = jnp.sum(values * values, axis=0, keepdims=True)
        return values * (lax.rsqrt(squares * (1.0 / HEAD_DIM) + EPS) * scale)

    def ask(head):
        asked = unit(head * HEAD_DIM, Q_SCALE).astype(BF16)
        keys = unit(E + head * HEAD_DIM, 1.0).T.astype(BF16)
        for at in blocks:
            scores[lax.rem(head, 2), at, : at.stop - at.start] = jnp.dot(
                keys[at, :], asked[:, at], preferred_element_type=F32
            )

    def answer(head):
        values = raw[pl.ds(pl.multiple_of(2 * E + head * HEAD_DIM, 8), HEAD_DIM), :].astype(BF16)
        for at in blocks:
            weights = jnp.exp2(scores[lax.rem(head, 2), at, : at.stop - at.start])
            if mask is not None:
                weights = jnp.where(mask, weights, 0.0)
            inverse = 1.0 / jnp.sum(weights, axis=0, keepdims=True)
            mixed = jnp.dot(values[:, at], weights.astype(BF16), preferred_element_type=F32)
            heads[pl.ds(pl.multiple_of(head * HEAD_DIM, 8), HEAD_DIM), at] = mixed * inverse

    def one_head(head, _):
        ask(head + 1)
        answer(head)
        return _

    ask(0)
    lax.fori_loop(0, HEADS - 1, one_head, 0, unroll=UNROLL)
    answer(HEADS - 1)


def kernel(
    lat_hbm, time_hbm, size_hbm, mod_hbm, w1_hbm, o1_hbm, w2_hbm, o2_hbm,
    out_hbm, change_ref,
    time_ref, size_ref, lat, mod, w1, o1, w2, o2, cond, inputs, raw, scores, heads,
    following, after, anchor, mine, drift, x_in, total, z_in, carry, c_in, done, u_in, out,
    part, parts,
    local_sem, next_send, next_recv, anchor_send, anchor_recv, y_send, y_recv,
    x_send, x_recv, z_send, z_recv, c_send, c_recv, u_send, u_recv, p_send, p_recv, out_sem,
):
    me = lax.axis_index("step")
    s = lax.axis_index("seq")
    z, x = me // NX, lax.rem(me, NX)
    fh, cg = x // 2, lax.rem(x, 2)

    loads = [
        pltpu.make_async_copy(src, dst, local_sem.at[i])
        for i, (src, dst) in enumerate(
            [
                (lat_hbm, lat), (mod_hbm, mod), (w1_hbm, w1), (o1_hbm, o1), (w2_hbm, w2), (o2_hbm, o2),
                (time_hbm, time_ref), (size_hbm, size_ref),
            ]
        )
    ]
    for load in loads:
        load.start()

    def to(step, seq):
        return {"step": step, "seq": seq}

    barrier = pltpu.get_barrier_semaphore()
    before = lax.rem(me + NX * NZ - 1, NX * NZ)
    behind = lax.rem(me + 1, NX * NZ)

    def greet_plane(k, _):
        other_s = lax.rem(s + lax.rem(k, NS), NS)
        other_x = lax.rem(x + k // NS, NX)
        pl.semaphore_signal(barrier, inc=1, device_id=to(z * NX + other_x, other_s), device_id_type=MESH)
        return _

    lax.fori_loop(1, NX * NS, greet_plane, 0)

    def greet_planes(k, _):
        other_z = lax.rem(z + k, NZ)
        pl.semaphore_signal(barrier, inc=1, device_id=to(other_z * NX + x, s), device_id_type=MESH)
        return _

    lax.fori_loop(1, NZ, greet_planes, 0)
    for step in (before, behind):
        pl.semaphore_signal(barrier, inc=1, device_id=to(step, s), device_id_type=MESH)

    loads[6].wait()
    loads[7].wait()
    loads[1].wait()
    one_hot = (lax.broadcasted_iota(jnp.int32, (16, mod.shape[0]), 1) == time_ref[0]).astype(BF16)
    cond[...] = jnp.dot(one_hot, mod[...], preferred_element_type=F32)[:8]

    def vector(i):
        return cond[0:1, i * D : (i + 1) * D]

    def condition(src, shift, scale):
        def some(i, _):
            rows = pl.ds(pl.multiple_of(i * NORM_ROWS, NORM_ROWS), NORM_ROWS)
            normal = layer_norm(src[rows, :].astype(F32))
            inputs[rows, :] = (normal * (1.0 + vector(scale)) + vector(shift)).astype(BF16)
            return _

        lax.fori_loop(0, ROWS // NORM_ROWS, some, 0)

    def piece(k, half):
        return pl.ds(pl.multiple_of(half * HALF + k * PIECE, PIECE), PIECE)

    def y_start(src, dst, send, recv, half):
        def start(k, _):
            target = lax.rem(s + k, NS)
            pltpu.make_async_remote_copy(
                src_ref=src.at[piece(target, half), :], dst_ref=dst.at[piece(s, half), :],
                send_sem=send, recv_sem=recv, device_id=to(me, target), device_id_type=MESH,
            ).start()
            return _

        lax.fori_loop(1, NS, start, 0)
        dst[piece(s, half), :] = src[piece(s, half), :]

    def moved(ref, sem):
        pltpu.make_async_copy(ref, ref, sem).wait()

    loads[0].wait()
    condition(lat, 0, 1)
    pl.semaphore_wait(barrier, NX * NS - 1 + NZ - 1 + 2)

    @pl.when(me == 0)
    def _():
        for half in range(2):
            y_start(lat, anchor, anchor_send, anchor_recv, half)

    send_next = pltpu.make_async_remote_copy(
        src_ref=lat, dst_ref=following, send_sem=next_send, recv_sem=next_recv,
        device_id=to(before, s), device_id_type=MESH,
    )
    send_next.start()

    contract_last = (((1,), (1,)), ((), ()))
    contract_first = (((0,), (0,)), ((), ()))
    halves = [slice(half * HALF, (half + 1) * HALF) for half in range(2)]

    def project(weights):
        def some(i, _):
            rows = pl.ds(pl.multiple_of(i * PROJECT, 16), PROJECT)
            raw[rows, :] = lax.dot_general(
                weights[rows, :], inputs[...], contract_last, preferred_element_type=F32
            )
            return _

        lax.fori_loop(0, 3 * E // PROJECT, some, 0)

    loads[2].wait()
    project(w1)
    attend(raw, heads, scores, (slice(0, ROWS),), None)
    loads[3].wait()

    def spatial_out(half, _):
        rows = pl.ds(pl.multiple_of(half * HALF, HALF), HALF)
        shown = lax.dot_general(
            heads[:, rows].astype(BF16), o1[...], contract_first, preferred_element_type=F32
        )
        after[rows, :] = (lat[rows, :].astype(F32) + vector(2) * shown).astype(BF16)
        y_start(after, mine, y_send, y_recv.at[half], half)
        return _

    lax.fori_loop(0, 2, spatial_out, 0, unroll=2)
    loads[4].wait()
    loads[5].wait()

    def block(half, holder):
        row = pl.multiple_of(half * HALF + (holder // 2) * QUART, QUART)
        col = pl.multiple_of(lax.rem(holder, 2) * SHIFT, 128)
        return pl.ds(row, QUART), pl.ds(col, WIDE)

    def x_start(half):
        for k in range(1, NX):
            target = lax.rem(x + k, NX)
            pltpu.make_async_remote_copy(
                src_ref=drift.at[block(half, target)], dst_ref=x_in.at[half, x],
                send_sem=x_send, recv_sem=x_recv.at[half],
                device_id=to(z * NX + target, s), device_id_type=MESH,
            ).start()
        x_in[half, x] = drift[block(half, x)]

    for half in range(2):
        moved(mine.at[pl.ds(half * HALF, HALF - PIECE), :], y_recv.at[half])
    condition(mine, 3, 4)
    project(w2)
    patch = lax.rem(lax.broadcasted_iota(jnp.int32, (HALF, HALF), 0), PIECE)
    patch_of_key = lax.rem(lax.broadcasted_iota(jnp.int32, (HALF, HALF), 1), PIECE)
    attend(raw, heads, scores, halves, patch == patch_of_key)

    @pl.when(me == 0)
    def _():
        moved(anchor.at[pl.ds(0, ROWS - 2 * PIECE), :], anchor_recv)

    def temporal_out(half, held):
        rows = pl.ds(pl.multiple_of(half * HALF, HALF), HALF)
        shown = lax.dot_general(
            heads[:, rows].astype(BF16), o2[...], contract_first, preferred_element_type=F32
        )
        drift[rows, :] = (size_ref[0] * (mine[rows, :].astype(F32) + vector(5) * shown)).astype(BF16)

        @pl.when(me == 0)
        def _():
            drift[rows, :] = (drift[rows, :].astype(F32) + anchor[rows, :].astype(F32)).astype(BF16)

        x_start(half)
        return held

    lax.fori_loop(0, 2, temporal_out, 0, unroll=2)

    for half in range(2):
        moved(x_in.at[half, pl.ds(0, NX - 1)], x_recv.at[half])
        block_sum = x_in[half, 0].astype(F32)
        for k in range(1, NX):
            block_sum = block_sum + x_in[half, k].astype(F32)
        total[half] = block_sum.astype(BF16).reshape(4, PIECE, WIDE)
        for frame in range(4):
            target = 2 * frame + half

            @pl.when(z != target)
            def _():
                pltpu.make_async_remote_copy(
                    src_ref=total.at[half, frame], dst_ref=z_in.at[z],
                    send_sem=z_send, recv_sem=z_recv,
                    device_id=to(target * NX + x, s), device_id_type=MESH,
                ).start()

            @pl.when(z == target)
            def _():
                z_in[z] = total[half, frame]

    for half in range(2):

        @pl.when(lax.rem(z, 2) == half)
        def _():
            moved(z_in.at[pl.ds(0, NZ - 1)], z_recv)
            running = jnp.zeros((PIECE, WIDE), F32)
            for k in range(NZ):
                carry[k] = running.astype(BF16)
                running = running + z_in[k].astype(F32)
            for k in range(1, NZ):
                target = lax.rem(z + k, NZ)
                pltpu.make_async_remote_copy(
                    src_ref=carry.at[target], dst_ref=c_in.at[half, z // 2],
                    send_sem=c_send, recv_sem=c_recv.at[half],
                    device_id=to(target * NX + x, s), device_id_type=MESH,
                ).start()
            c_in[half, z // 2] = carry[z]

    for half in range(2):

        @pl.when(lax.rem(z, 2) == half)
        def _():
            moved(c_in.at[half, pl.ds(0, 3)], c_recv.at[half])

        @pl.when(lax.rem(z, 2) != half)
        def _():
            moved(c_in.at[half], c_recv.at[half])

        running = c_in[half].astype(F32).reshape(QUART, WIDE)
        for k in range(NX):
            running = running + x_in[half, k].astype(F32)
            done[half, k] = running.astype(BF16).reshape(4, PIECE, WIDE)

        def u_start(k, held):
            x_to, frame = lax.rem(x + k // 4, NX), lax.rem(k, 4)

            @pl.when(jnp.logical_or(x_to != x, fh * 4 + frame != s))
            def _():
                pltpu.make_async_remote_copy(
                    src_ref=done.at[half, x_to, frame], dst_ref=u_in.at[cg, piece(s, half), :],
                    send_sem=u_send, recv_sem=u_recv.at[half],
                    device_id=to(z * NX + x_to, fh * 4 + frame), device_id_type=MESH,
                ).start()

            return held

        lax.fori_loop(0, NX * 4, u_start, 0)

        @pl.when(s // 4 == fh)
        def _():
            u_in[cg, piece(s, half), :] = done[half, x, lax.rem(s, 4)]

    send_next.wait_recv()
    known = jnp.where(me == NX * NZ - 1, 0.0, 1.0)
    part[...] = jnp.zeros_like(part)
    stores = []
    for half in range(2):
        rows = halves[half]

        @pl.when(s // 4 == fh)
        def _():
            moved(u_in.at[0, pl.ds(0, ROWS - PIECE), :], u_recv.at[half])

        @pl.when(s // 4 != fh)
        def _():
            moved(u_in.at[0], u_recv.at[half])

        out[rows, :WIDE] = u_in[0, rows, :]
        out[rows, WIDE:] = u_in[1, rows, 128:]
        store = pltpu.make_async_copy(out.at[rows, :], out_hbm.at[rows, :], out_sem.at[half])
        store.start()
        stores.append(store)
        goal = jnp.where(known > 0.5, following[rows, :].astype(F32), 0.0)
        difference = out[rows, :].astype(F32) - goal
        squares = (difference * difference).reshape(HALF // 8, 8, D).sum(axis=0)
        for t in range(D // 128):
            part[...] += squares[:, t * 128 : (t + 1) * 128]

    for k in range(1, NS):
        pltpu.make_async_remote_copy(
            src_ref=part, dst_ref=parts.at[s], send_sem=p_send, recv_sem=p_recv,
            device_id=to(me, lax.rem(s + k, NS)), device_id_type=MESH,
        ).start()
    parts[s] = part[...]
    moved(parts.at[pl.ds(0, NS - 1)], p_recv)
    change_ref[0] = jnp.sum(jnp.sum(parts[...], axis=0)) * (1.0 / (NS * ROWS * D))

    send_next.wait_send()

    @pl.when(me == 0)
    def _():
        moved(anchor.at[pl.ds(0, ROWS - 2 * PIECE), :], anchor_send)

    moved(mine.at[pl.ds(0, ROWS - 2 * PIECE), :], y_send)
    moved(x_in.at[:, pl.ds(0, NX - 1)], x_send)
    moved(z_in.at[pl.ds(0, NZ - 1)], z_send)
    moved(carry.at[pl.ds(0, NZ - 1)], c_send)

    @pl.when(s // 4 == fh)
    def _():
        moved(u_in.at[:, pl.ds(0, ROWS - PIECE), :], u_send)

    @pl.when(s // 4 != fh)
    def _():
        moved(u_in, u_send)

    moved(parts.at[pl.ds(0, NS - 1)], p_send)
    for store in stores:
        store.wait()


def body(latents, timesteps, step_sizes, modulation, spatial_qkv, spatial_out, temporal_qkv, temporal_out):
    dma = pltpu.SemaphoreType.DMA

    def vmem(*shape, dtype=BF16):
        return pltpu.VMEM(shape, dtype)

    table = modulation.shape[0]
    updated, change = pl.pallas_call(
        kernel,
        out_shape=(jax.ShapeDtypeStruct((ROWS, D), BF16), jax.ShapeDtypeStruct((1,), F32)),
        in_specs=[pl.BlockSpec(memory_space=pltpu.HBM)] * 8,
        out_specs=(pl.BlockSpec(memory_space=pl.ANY), pl.BlockSpec(memory_space=pltpu.SMEM)),
        scratch_shapes=[
            pltpu.SMEM((1,), jnp.int32), pltpu.SMEM((1,), F32),
            vmem(ROWS, D), vmem(table, 6 * D),
            vmem(3 * E, D), vmem(E, D), vmem(3 * E, D), vmem(E, D),
            vmem(8, 6 * D, dtype=F32), vmem(ROWS, D),
            vmem(3 * E, ROWS, dtype=F32), vmem(2, ROWS, ROWS, dtype=F32), vmem(E, ROWS, dtype=F32),
            vmem(ROWS, D), vmem(ROWS, D), vmem(ROWS, D), vmem(ROWS, D), vmem(ROWS, D),
            vmem(2, NX, QUART, WIDE), vmem(2, 4, PIECE, WIDE), vmem(NZ, PIECE, WIDE),
            vmem(NZ, PIECE, WIDE), vmem(2, 4, PIECE, WIDE),
            vmem(2, NX, 4, PIECE, WIDE), vmem(2, ROWS, WIDE), vmem(ROWS, D),
            vmem(8, 128, dtype=F32), vmem(NS, 8, 128, dtype=F32),
            dma((8,)), dma, dma, dma, dma, dma, dma((2,)),
            dma, dma((2,)), dma, dma, dma, dma((2,)), dma, dma((2,)), dma, dma, dma((2,)),
        ],
        compiler_params=pltpu.CompilerParams(
            collective_id=0, has_side_effects=True, vmem_limit_bytes=40 * 1024 * 1024
        ),
        cost_estimate=pl.CostEstimate(
            flops=2800000000, bytes_accessed=12000000, transcendentals=1000000
        ),
    )(
        latents.reshape(ROWS, D), timesteps, step_sizes, modulation,
        spatial_qkv.T, spatial_out, temporal_qkv.T, temporal_out,
    )
    return updated[None, None], change


def solution(mesh):
    in_specs = (P("step", "seq", None, None), P("step"), P("step"), P(), P(), P(), P(), P())
    out_specs = (P("step", "seq", None, None), P("step"))
    return jax.shard_map(body, mesh=mesh, in_specs=in_specs, out_specs=out_specs, check_vma=False)
```

```python
import math

import jax
import jax.numpy as jnp
from jax import lax
from jax.experimental import pallas as pl
from jax.experimental.pallas import tpu as pltpu
from jax.sharding import PartitionSpec as P

UNROLL = 7
PROJECT = 864
MESH = pl.DeviceIdType.MESH
F32 = jnp.float32
BF16 = jnp.bfloat16

D = 1152
HEADS = 8
HEAD_DIM = 72
E = HEADS * HEAD_DIM
ROWS = 256
HALF = 128
PIECE = 8
NX = 4
NZ = 8
NS = 8
STEP_ROWS = NS * PIECE
EPS = 1e-6
LOG2E = 1.4426950408889634
Q_SCALE = 3.0 / math.sqrt(HEAD_DIM) * LOG2E


def layer_norm(values):
    center = values - jnp.mean(values, axis=-1, keepdims=True)
    spread = jnp.mean(center * center, axis=-1, keepdims=True)
    return center * lax.rsqrt(spread + EPS)


def attend(raw, heads, scores, blocks, mask):
    def unit(start, scale):
        values = raw[pl.ds(pl.multiple_of(start, 8), HEAD_DIM), :]
        squares = jnp.sum(values * values, axis=0, keepdims=True)
        return values * (lax.rsqrt(squares * (1.0 / HEAD_DIM) + EPS) * scale)

    def ask(head):
        asked = unit(head * HEAD_DIM, Q_SCALE).astype(BF16)
        keys = unit(E + head * HEAD_DIM, 1.0).T.astype(BF16)
        for at in blocks:
            scores[lax.rem(head, 2), at, : at.stop - at.start] = jnp.dot(
                keys[at, :], asked[:, at], preferred_element_type=F32
            )

    def answer(head):
        values = raw[pl.ds(pl.multiple_of(2 * E + head * HEAD_DIM, 8), HEAD_DIM), :].astype(BF16)
        for at in blocks:
            weights = jnp.exp2(scores[lax.rem(head, 2), at, : at.stop - at.start])
            if mask is not None:
                weights = jnp.where(mask, weights, 0.0)
            inverse = 1.0 / jnp.sum(weights, axis=0, keepdims=True)
            mixed = jnp.dot(values[:, at], weights.astype(BF16), preferred_element_type=F32)
            heads[pl.ds(pl.multiple_of(head * HEAD_DIM, 8), HEAD_DIM), at] = mixed * inverse

    def one_head(head, _):
        ask(head + 1)
        answer(head)
        return _

    ask(0)
    lax.fori_loop(0, HEADS - 1, one_head, 0, unroll=UNROLL)
    answer(HEADS - 1)


def kernel(
    lat_hbm, time_hbm, size_hbm, mod_hbm, w1_hbm, o1_hbm, w2_hbm, o2_hbm,
    out, change_ref,
    time_ref, size_ref, lat, mod, w1, o1, w2, o2, cond, inputs, raw, scores, heads,
    after, mine, temper, following, drift, total, z_in, carry, c_in, done, part, parts,
    local_sem, temper_send, temper_recv, y_send, y_recv, next_send, next_recv,
    z_send, z_recv, c_send, c_recv, u_send, u_recv, p_send, p_recv, own_sem,
):
    me = lax.axis_index("step")
    s = lax.axis_index("seq")
    z, x = me // NX, lax.rem(me, NX)

    loads = [
        pltpu.make_async_copy(src, dst, local_sem.at[i])
        for i, (src, dst) in enumerate(
            [
                (mod_hbm, mod), (lat_hbm, lat), (w1_hbm, w1), (o1_hbm, o1), (w2_hbm, w2), (o2_hbm, o2),
                (time_hbm, time_ref), (size_hbm, size_ref),
            ]
        )
    ]
    for i in (6, 7, 0, 1, 2, 3, 4, 5):
        loads[i].start()

    def to(step, seq):
        return {"step": step, "seq": seq}

    def greet(step, seq):
        pl.semaphore_signal(barrier, inc=1, device_id=to(step, seq), device_id_type=MESH)

    barrier = pltpu.get_barrier_semaphore()

    def greet_plane(k, _):
        greet(z * NX + lax.rem(x + k // NS, NX), lax.rem(s + lax.rem(k, NS), NS))
        return _

    lax.fori_loop(1, NX * NS, greet_plane, 0)

    def greet_planes(k, _):
        greet(lax.rem(z + k, NZ) * NX + x, s)
        return _

    lax.fori_loop(1, NZ, greet_planes, 0)

    @pl.when(z < NZ - 1)
    def _():
        def greet_next(k, held):
            greet((z + 1) * NX, lax.rem(s + k, NS))
            return held

        lax.fori_loop(0, NS, greet_next, 0)

    loads[6].wait()
    loads[7].wait()
    loads[0].wait()
    one_hot = (lax.broadcasted_iota(jnp.int32, (16, mod.shape[0]), 1) == time_ref[0]).astype(BF16)
    cond[...] = jnp.dot(one_hot, mod[...], preferred_element_type=F32)[:8]

    def vector(i):
        return cond[0:1, i * D : (i + 1) * D]

    temper[x] = jnp.concatenate(
        [vector(3), 1.0 + vector(4), vector(5) * size_ref[0], jnp.broadcast_to(size_ref[0], (5, D))], axis=0
    )

    def moved(ref, sem):
        pltpu.make_async_copy(ref, ref, sem).wait()

    def normal_in(src, i, shift, scale, pieces):
        rows = pl.ds(pl.multiple_of(i * pieces * PIECE, pieces * PIECE), pieces * PIECE)
        values = src[pl.ds(i * pieces, pieces)].astype(F32).reshape(pieces * PIECE, D)
        inputs[rows, :] = (layer_norm(values) * scale + shift).astype(BF16)

    loads[1].wait()

    def spatial_in(i, _):
        normal_in(lat, i, vector(0), 1.0 + vector(1), 16)
        return _

    lax.fori_loop(0, 2, spatial_in, 0)

    contract_last = (((1,), (1,)), ((), ()))
    contract_first = (((0,), (0,)), ((), ()))

    def project(weights):
        def some(i, _):
            rows = pl.ds(pl.multiple_of(i * PROJECT, 16), PROJECT)
            raw[rows, :] = lax.dot_general(
                weights[rows, :], inputs[...], contract_last, preferred_element_type=F32
            )
            return _

        lax.fori_loop(0, 3 * E // PROJECT, some, 0)

    loads[2].wait()
    project(w1)
    attend(raw, heads, scores, (slice(0, ROWS),), None)
    loads[3].wait()

    @pl.when(jnp.logical_and(x == 0, z > 0))
    def _():
        pl.semaphore_wait(barrier, 2 * NX * NS - 1 + NZ - 1)

    @pl.when(jnp.logical_not(jnp.logical_and(x == 0, z > 0)))
    def _():
        pl.semaphore_wait(barrier, NX * NS - 1 + NZ - 1)

    def place(x_at, s_at):
        return lax.rem(s_at, 2) * 16 + (s_at // 2) * 4 + x_at

    own = place(x, s)

    for k in range(1, NX):
        pltpu.make_async_remote_copy(
            src_ref=temper.at[x], dst_ref=temper.at[x], send_sem=temper_send, recv_sem=temper_recv,
            device_id=to(z * NX + lax.rem(x + k, NX), s), device_id_type=MESH,
        ).start()

    for half in range(2):
        rows = slice(half * HALF, (half + 1) * HALF)
        pieces = slice(half * 16, (half + 1) * 16)
        shown = lax.dot_general(
            heads[:, rows].astype(BF16), o1[...], contract_first, preferred_element_type=F32
        )
        state = lat[pieces].astype(F32).reshape(HALF, D)
        after[pieces] = (state + vector(2) * shown).reshape(16, PIECE, D).astype(BF16)

        def y_start(k, _):
            x_to = lax.rem(x + k // 4, NX)
            s_to = lax.rem(s // 2 + lax.rem(k, 4), 4) * 2 + half

            @pl.when(jnp.logical_or(x_to != x, s_to != s))
            def _():
                pltpu.make_async_remote_copy(
                    src_ref=after.at[place(x_to, s_to)], dst_ref=mine.at[x * NS + s],
                    send_sem=y_send, recv_sem=y_recv,
                    device_id=to(z * NX + x_to, s_to), device_id_type=MESH,
                ).start()

            return k

        lax.fori_loop(0, 16, y_start, 0)
    mine[x * NS + s] = after[own]

    first = me == 0
    plane = jnp.where(jnp.logical_and(x == 0, z > 0), z - 1, z)
    slot = jnp.where(first, NX, lax.rem(x + NX - 1, NX))
    kind = jnp.where(first, 2, jnp.where(x == 0, 1, 0))

    def next_start(k, _):
        x_to, s_to = lax.rem(x + k // NS, NX), lax.rem(s + lax.rem(k, NS), NS)
        pltpu.make_async_remote_copy(
            src_ref=lat.at[place(x_to, s_to)], dst_ref=following.at[slot, s],
            send_sem=next_send, recv_sem=next_recv.at[kind],
            device_id=to(plane * NX + x_to, s_to), device_id_type=MESH,
        ).start()
        return _

    lax.fori_loop(1, NX * NS, next_start, 0)

    @pl.when(plane != z)
    def _():
        next_start(0, 0)

    @pl.when(plane == z)
    def _():
        following[slot, s] = lat[own]

    @pl.when(z == NZ - 1)
    def _():
        following[NX - 1] = jnp.zeros(following.shape[1:], BF16)

    loads[4].wait()
    loads[5].wait()
    moved(temper.at[pl.ds(0, NX - 1)], temper_recv)
    moved(mine.at[pl.ds(0, NX * NS - 1)], y_recv)

    def temporal_in(i, _):
        normal_in(mine, i, temper[i, 0:1, :], temper[i, 1:2, :], NS)
        return _

    lax.fori_loop(0, NX, temporal_in, 0, unroll=2)
    project(w2)
    row = lax.broadcasted_iota(jnp.int32, (HALF, HALF), 0)
    col = lax.broadcasted_iota(jnp.int32, (HALF, HALF), 1)
    same = jnp.logical_and(row // STEP_ROWS == col // STEP_ROWS, lax.rem(row, PIECE) == lax.rem(col, PIECE))
    attend(raw, heads, scores, (slice(0, HALF), slice(HALF, ROWS)), same)
    for half in range(2):
        rows = slice(half * HALF, (half + 1) * HALF)
        shown = lax.dot_general(
            heads[:, rows].astype(BF16), o2[...], contract_first, preferred_element_type=F32
        )
        for i in range(2):
            step = half * 2 + i
            state = mine[step * NS : (step + 1) * NS].astype(F32).reshape(STEP_ROWS, D)
            drift[step] = (
                state * temper[step, 3:4, :]
                + temper[step, 2:3, :] * shown[i * STEP_ROWS : (i + 1) * STEP_ROWS]
            )

    @pl.when(z == 0)
    def _():
        @pl.when(first)
        def _():
            moved(following.at[NX, pl.ds(0, NS - 1)], next_recv.at[2])

        @pl.when(jnp.logical_not(first))
        def _():
            moved(following.at[NX], next_recv.at[2])

        drift[0] = drift[0] + following[NX].astype(F32).reshape(STEP_ROWS, D)

    everything = drift[0] + drift[1] + drift[2] + drift[3]
    total[...] = everything.reshape(NS, PIECE, D).astype(BF16)

    def z_start(k, _):
        target = lax.rem(z + k, NZ)
        pltpu.make_async_remote_copy(
            src_ref=total.at[target], dst_ref=z_in.at[z], send_sem=z_send, recv_sem=z_recv,
            device_id=to(target * NX + x, s), device_id_type=MESH,
        ).start()
        return _

    lax.fori_loop(1, NZ, z_start, 0)
    z_in[z] = total[z]
    moved(z_in.at[pl.ds(0, NZ - 1)], z_recv)
    running = jnp.zeros((PIECE, D), F32)
    for k in range(NZ):
        carry[k] = running.astype(BF16)
        running = running + z_in[k].astype(F32)

    def c_start(k, held):
        target = lax.rem(z + k, NZ)

        @pl.when(target > 0)
        def _():
            pltpu.make_async_remote_copy(
                src_ref=carry.at[target], dst_ref=c_in.at[z], send_sem=c_send, recv_sem=c_recv,
                device_id=to(target * NX + x, s), device_id_type=MESH,
            ).start()

        return held

    lax.fori_loop(1, NZ, c_start, 0)

    @pl.when(z == 0)
    def _():
        c_in[...] = jnp.zeros(c_in.shape, BF16)

    @pl.when(z > 0)
    def _():
        c_in[z] = carry[z]
        moved(c_in.at[pl.ds(0, NZ - 1)], c_recv)

    running = c_in[...].astype(F32).reshape(STEP_ROWS, D)
    for step in range(NX):
        running = running + drift[step]
        done[step] = running.reshape(NS, PIECE, D).astype(BF16)

    def u_start(k, _):
        x_to, s_to = lax.rem(x + k // NS, NX), lax.rem(s + lax.rem(k, NS), NS)
        pltpu.make_async_remote_copy(
            src_ref=done.at[x_to, s_to], dst_ref=out.at[own], send_sem=u_send, recv_sem=u_recv,
            device_id=to(z * NX + x_to, s_to), device_id_type=MESH,
        ).start()
        return _

    lax.fori_loop(1, NX * NS, u_start, 0)
    keep = pltpu.make_async_copy(done.at[x, s], out.at[own], own_sem)
    keep.start()

    @pl.when(x == 0)
    def _():
        moved(following.at[pl.ds(0, NX - 1)], next_recv.at[0])

    @pl.when(x > 0)
    def _():
        moved(mine.at[pl.ds(0, (NX - 1) * NS - 1)], next_recv.at[0])

    @pl.when(z < NZ - 1)
    def _():
        moved(following.at[0], next_recv.at[1])

    for step in range(NX):
        difference = done[step].astype(F32) - following[step].astype(F32)
        squares = jnp.sum(difference * difference, axis=0)
        tile = squares[:, :128]
        for t in range(1, D // 128):
            tile = tile + squares[:, t * 128 : (t + 1) * 128]
        part[step] = tile

    def p_start(k, _):
        x_to, s_to = lax.rem(x + k // NS, NX), lax.rem(s + lax.rem(k, NS), NS)
        pltpu.make_async_remote_copy(
            src_ref=part.at[x_to], dst_ref=parts.at[x * NS + s], send_sem=p_send, recv_sem=p_recv,
            device_id=to(z * NX + x_to, s_to), device_id_type=MESH,
        ).start()
        return _

    lax.fori_loop(1, NX * NS, p_start, 0)
    parts[x * NS + s] = part[x]

    moved(temper.at[pl.ds(0, NX - 1)], temper_send)
    moved(mine.at[pl.ds(0, NX * NS - 1)], y_send)

    @pl.when(plane != z)
    def _():
        moved(mine, next_send)

    @pl.when(plane == z)
    def _():
        moved(mine.at[pl.ds(0, NX * NS - 1)], next_send)

    moved(z_in.at[pl.ds(0, NZ - 1)], z_send)

    @pl.when(z == 0)
    def _():
        moved(carry.at[pl.ds(0, NZ - 1)], c_send)

    @pl.when(z > 0)
    def _():
        moved(carry.at[pl.ds(0, NZ - 2)], c_send)

    keep.wait()
    moved(mine.at[pl.ds(0, NX * NS - 1)], u_send)
    moved(parts.at[pl.ds(0, NX * NS - 1)], p_send)
    moved(mine.at[pl.ds(0, NX * NS - 1)], u_recv)
    moved(parts.at[pl.ds(0, NX * NS - 1)], p_recv)
    change_ref[0] = jnp.sum(jnp.sum(parts[...], axis=0)) * (1.0 / (NS * ROWS * D))


def body(latents, timesteps, step_sizes, modulation, spatial_qkv, spatial_out, temporal_qkv, temporal_out):
    dma = pltpu.SemaphoreType.DMA

    def vmem(*shape, dtype=BF16):
        return pltpu.VMEM(shape, dtype)

    def pieces(*count):
        return pltpu.VMEM((count or (NX * NS,)) + (PIECE, D), BF16)

    table = modulation.shape[0]
    updated, change = pl.pallas_call(
        kernel,
        out_shape=(jax.ShapeDtypeStruct((NX * NS, PIECE, D), BF16), jax.ShapeDtypeStruct((1,), F32)),
        in_specs=[pl.BlockSpec(memory_space=pl.ANY)] * 8,
        out_specs=(pl.BlockSpec(memory_space=pl.ANY), pl.BlockSpec(memory_space=pltpu.SMEM)),
        scratch_shapes=[
            pltpu.SMEM((1,), jnp.int32), pltpu.SMEM((1,), F32),
            pieces(), vmem(table, 6 * D),
            vmem(3 * E, D), vmem(E, D), vmem(3 * E, D), vmem(E, D),
            vmem(8, 6 * D, dtype=F32), vmem(ROWS, D),
            vmem(3 * E, ROWS, dtype=F32), vmem(2, ROWS, ROWS, dtype=F32), vmem(E, ROWS, dtype=F32),
            pieces(), pieces(), vmem(NX, 8, D, dtype=F32), pieces(NX + 1, NS),
            vmem(NX, STEP_ROWS, D, dtype=F32),
            pieces(NZ), pieces(NZ), pieces(NZ), pieces(NZ), pieces(NX, NS),
            vmem(NX, 8, 128, dtype=F32), vmem(NX * NS, 8, 128, dtype=F32),
            dma((8,)), dma, dma, dma, dma, dma, dma((3,)),
            dma, dma, dma, dma, dma, dma, dma, dma, dma,
        ],
        compiler_params=pltpu.CompilerParams(
            collective_id=0, has_side_effects=True, vmem_limit_bytes=56 * 1024 * 1024
        ),
        cost_estimate=pl.CostEstimate(
            flops=2800000000, bytes_accessed=12000000, transcendentals=1000000
        ),
    )(
        latents.reshape(NX * NS, PIECE, D), timesteps, step_sizes, modulation,
        spatial_qkv.T, spatial_out, temporal_qkv.T, temporal_out,
    )
    return updated.reshape(latents.shape), change


def solution(mesh):
    in_specs = (P("step", "seq", None, None), P("step"), P("step"), P(), P(), P(), P(), P())
    out_specs = (P("step", "seq", None, None), P("step"))
    return jax.shard_map(body, mesh=mesh, in_specs=in_specs, out_specs=out_specs, check_vma=False)
```

```python
import math

import jax
import jax.numpy as jnp
from jax import lax
from jax.experimental import pallas as pl
from jax.experimental.pallas import tpu as pltpu
from jax.sharding import PartitionSpec as P

UNROLL = 7
PROJECT = 864
MESH = pl.DeviceIdType.MESH
F32 = jnp.float32
BF16 = jnp.bfloat16

D = 1152
HEADS = 8
HEAD_DIM = 72
E = HEADS * HEAD_DIM
ROWS = 256
HALF = 128
PIECE = 8
NX = 4
NZ = 8
NS = 8
STEP_ROWS = NS * PIECE
EPS = 1e-6
LOG2E = 1.4426950408889634
Q_SCALE = 3.0 / math.sqrt(HEAD_DIM) * LOG2E


NEAR_LAST = [
    (2, 2), (2, 1), (2, 3), (1, 2), (3, 2), (1, 1), (3, 3), (1, 3),
    (3, 1), (2, 0), (0, 2), (1, 0), (0, 1), (3, 0), (0, 3), (0, 0),
]
X_OFFSETS = sum(dx << (2 * j) for j, (dx, _) in enumerate(NEAR_LAST))
Y_OFFSETS = sum(dy << (2 * j) for j, (_, dy) in enumerate(NEAR_LAST))


def chip(j, x, y):
    dx = lax.rem(lax.shift_right_logical(jnp.int32(X_OFFSETS), 2 * j), 4)
    dy = lax.rem(lax.shift_right_logical(jnp.int32(Y_OFFSETS), 2 * j), 4)
    return lax.rem(x + dx, 4), lax.rem(y + dy, 4)


def other(j, x, s):
    x_to, y_to = chip(j // 2, x, s // 2)
    return x_to, y_to * 2 + lax.rem(s + 1 + lax.rem(j, 2), 2)


def other_plane(j, z):
    return lax.rem(z + NZ // 2 + (1 - 2 * lax.rem(j, 2)) * ((j + 1) // 2), NZ)


def layer_norm(values):
    center = values - jnp.mean(values, axis=-1, keepdims=True)
    spread = jnp.mean(center * center, axis=-1, keepdims=True)
    return center * lax.rsqrt(spread + EPS)


def attend(raw, heads, scores, blocks, mask):
    def unit(start, scale):
        values = raw[pl.ds(pl.multiple_of(start, 8), HEAD_DIM), :]
        squares = jnp.sum(values * values, axis=0, keepdims=True)
        return values * (lax.rsqrt(squares * (1.0 / HEAD_DIM) + EPS) * scale)

    def ask(head):
        asked = unit(head * HEAD_DIM, Q_SCALE).astype(BF16)
        keys = unit(E + head * HEAD_DIM, 1.0).T.astype(BF16)
        for at in blocks:
            scores[lax.rem(head, 2), at, : at.stop - at.start] = jnp.dot(
                keys[at, :], asked[:, at], preferred_element_type=F32
            )

    def answer(head):
        values = raw[pl.ds(pl.multiple_of(2 * E + head * HEAD_DIM, 8), HEAD_DIM), :].astype(BF16)
        for at in blocks:
            weights = jnp.exp2(scores[lax.rem(head, 2), at, : at.stop - at.start])
            if mask is not None:
                weights = jnp.where(mask, weights, 0.0)
            inverse = 1.0 / jnp.sum(weights, axis=0, keepdims=True)
            mixed = jnp.dot(values[:, at], weights.astype(BF16), preferred_element_type=F32)
            heads[pl.ds(pl.multiple_of(head * HEAD_DIM, 8), HEAD_DIM), at] = mixed * inverse

    def one_head(head, _):
        ask(head + 1)
        answer(head)
        return _

    ask(0)
    lax.fori_loop(0, HEADS - 1, one_head, 0, unroll=UNROLL)
    answer(HEADS - 1)


def kernel(
    lat_hbm, time_hbm, size_hbm, mod_hbm, w1_hbm, o1_hbm, w2_hbm, o2_hbm,
    out, parts,
    time_ref, size_ref, lat, mod, w1, o1, w2, o2, cond, inputs, raw, scores, heads,
    after, mine, temper, following, drift, total, z_in, carry, c_in, done, part,
    local_sem, temper_send, temper_recv, y_send, y_recv, next_send, next_recv,
    z_send, z_recv, c_send, c_recv, u_send, u_recv, p_send, p_recv, own_sem, own_part_sem,
):
    me = lax.axis_index("step")
    s = lax.axis_index("seq")
    z, x = me // NX, lax.rem(me, NX)

    loads = [
        pltpu.make_async_copy(src, dst, local_sem.at[i])
        for i, (src, dst) in enumerate(
            [
                (mod_hbm, mod), (lat_hbm, lat), (w1_hbm.at[pl.ds(0, PROJECT)], w1.at[pl.ds(0, PROJECT)]), (o1_hbm, o1), (w2_hbm, w2), (o2_hbm, o2),
                (time_hbm, time_ref), (size_hbm, size_ref),
                (w1_hbm.at[pl.ds(PROJECT, PROJECT)], w1.at[pl.ds(PROJECT, PROJECT)]),
            ]
        )
    ]
    for i in (6, 7, 0, 1, 2, 8, 3, 4, 5):
        loads[i].start()

    def to(step, seq):
        return {"step": step, "seq": seq}

    def greet(step, seq):
        pl.semaphore_signal(barrier, inc=1, device_id=to(step, seq), device_id_type=MESH)

    barrier = pltpu.get_barrier_semaphore()

    def greet_plane(k, _):
        greet(z * NX + lax.rem(x + k // NS, NX), lax.rem(s + lax.rem(k, NS), NS))
        return _

    lax.fori_loop(1, NX * NS, greet_plane, 0)

    def greet_planes(k, _):
        greet(lax.rem(z + k, NZ) * NX + x, s)
        return _

    lax.fori_loop(1, NZ, greet_planes, 0)

    @pl.when(z < NZ - 1)
    def _():
        def greet_next(k, held):
            greet((z + 1) * NX, lax.rem(s + k, NS))
            return held

        lax.fori_loop(0, NS, greet_next, 0)

    loads[6].wait()
    loads[7].wait()
    loads[0].wait()
    one_hot = (lax.broadcasted_iota(jnp.int32, (16, mod.shape[0]), 1) == time_ref[0]).astype(BF16)
    cond[...] = jnp.dot(one_hot, mod[...], preferred_element_type=F32)[:8]

    def vector(i):
        return cond[0:1, i * D : (i + 1) * D]

    temper[x] = jnp.concatenate(
        [vector(3), 1.0 + vector(4), vector(5) * size_ref[0], jnp.broadcast_to(size_ref[0], (5, D))], axis=0
    )

    def moved(ref, sem):
        pltpu.make_async_copy(ref, ref, sem).wait()

    def normal_in(src, i, shift, scale, pieces):
        rows = pl.ds(pl.multiple_of(i * pieces * PIECE, pieces * PIECE), pieces * PIECE)
        values = src[pl.ds(i * pieces, pieces)].astype(F32).reshape(pieces * PIECE, D)
        inputs[rows, :] = (layer_norm(values) * scale + shift).astype(BF16)

    loads[1].wait()

    def spatial_in(i, _):
        normal_in(lat, i, vector(0), 1.0 + vector(1), 16)
        return _

    lax.fori_loop(0, 2, spatial_in, 0)

    contract_last = (((1,), (1,)), ((), ()))
    contract_first = (((0,), (0,)), ((), ()))

    def project(weights, i):
        rows = pl.ds(pl.multiple_of(i * PROJECT, 16), PROJECT)
        raw[rows, :] = lax.dot_general(
            weights[rows, :], inputs[...], contract_last, preferred_element_type=F32
        )

    def first_project(i, _):
        @pl.when(i == 0)
        def _():
            loads[2].wait()

        @pl.when(i == 1)
        def _():
            loads[8].wait()

        project(w1, i)
        return i

    lax.fori_loop(0, 3 * E // PROJECT, first_project, 0)
    attend(raw, heads, scores, (slice(0, ROWS),), None)
    loads[3].wait()

    @pl.when(jnp.logical_and(x == 0, z > 0))
    def _():
        pl.semaphore_wait(barrier, 2 * NX * NS - 1 + NZ - 1)

    @pl.when(jnp.logical_not(jnp.logical_and(x == 0, z > 0)))
    def _():
        pl.semaphore_wait(barrier, NX * NS - 1 + NZ - 1)

    def place(x_at, s_at):
        return lax.rem(s_at, 2) * 16 + (s_at // 2) * 4 + x_at

    own = place(x, s)

    for k in range(1, NX):
        pltpu.make_async_remote_copy(
            src_ref=temper.at[x], dst_ref=temper.at[x], send_sem=temper_send, recv_sem=temper_recv,
            device_id=to(z * NX + lax.rem(x + k, NX), s), device_id_type=MESH,
        ).start()

    for half in range(2):
        rows = slice(half * HALF, (half + 1) * HALF)
        pieces = slice(half * 16, (half + 1) * 16)
        shown = lax.dot_general(
            heads[:, rows].astype(BF16), o1[...], contract_first, preferred_element_type=F32
        )
        state = lat[pieces].astype(F32).reshape(HALF, D)
        after[pieces] = (state + vector(2) * shown).reshape(16, PIECE, D).astype(BF16)

        def y_start(k, _):
            x_to, y_to = chip(k, x, s // 2)
            s_to = y_to * 2 + half

            @pl.when(jnp.logical_or(x_to != x, s_to != s))
            def _():
                pltpu.make_async_remote_copy(
                    src_ref=after.at[place(x_to, s_to)], dst_ref=mine.at[x * NS + s],
                    send_sem=y_send, recv_sem=y_recv,
                    device_id=to(z * NX + x_to, s_to), device_id_type=MESH,
                ).start()

            return k

        lax.fori_loop(0, 16, y_start, 0)
    mine[x * NS + s] = after[own]

    first = me == 0
    plane = jnp.where(jnp.logical_and(x == 0, z > 0), z - 1, z)
    slot = jnp.where(first, NX, lax.rem(x + NX - 1, NX))
    kind = jnp.where(first, 2, jnp.where(x == 0, 1, 0))

    def next_start(k, _):
        x_to, s_to = other(k, x, s)
        pltpu.make_async_remote_copy(
            src_ref=lat.at[place(x_to, s_to)], dst_ref=following.at[slot, s],
            send_sem=next_send, recv_sem=next_recv.at[kind],
            device_id=to(plane * NX + x_to, s_to), device_id_type=MESH,
        ).start()
        return _

    def next_all():
        lax.fori_loop(0, NX * NS - 1, next_start, 0)

        @pl.when(plane != z)
        def _():
            next_start(NX * NS - 1, 0)

        @pl.when(plane == z)
        def _():
            following[slot, s] = lat[own]

    pl.when(first)(next_all)

    @pl.when(z == NZ - 1)
    def _():
        following[NX - 1] = jnp.zeros(following.shape[1:], BF16)

    loads[4].wait()
    loads[5].wait()
    moved(temper.at[pl.ds(0, NX - 1)], temper_recv)
    moved(mine.at[pl.ds(0, NX * NS - 1)], y_recv)

    def temporal_in(i, _):
        normal_in(mine, i, temper[i, 0:1, :], temper[i, 1:2, :], NS)
        return _

    lax.fori_loop(0, NX, temporal_in, 0, unroll=2)

    def second_project(i, _):
        project(w2, i)
        return _

    lax.fori_loop(0, 3 * E // PROJECT, second_project, 0)
    row = lax.broadcasted_iota(jnp.int32, (HALF, HALF), 0)
    col = lax.broadcasted_iota(jnp.int32, (HALF, HALF), 1)
    same = jnp.logical_and(row // STEP_ROWS == col // STEP_ROWS, lax.rem(row, PIECE) == lax.rem(col, PIECE))
    attend(raw, heads, scores, (slice(0, HALF), slice(HALF, ROWS)), same)
    for half in range(2):
        rows = slice(half * HALF, (half + 1) * HALF)
        shown = lax.dot_general(
            heads[:, rows].astype(BF16), o2[...], contract_first, preferred_element_type=F32
        )
        for i in range(2):
            step = half * 2 + i
            state = mine[step * NS : (step + 1) * NS].astype(F32).reshape(STEP_ROWS, D)
            drift[step] = (
                state * temper[step, 3:4, :]
                + temper[step, 2:3, :] * shown[i * STEP_ROWS : (i + 1) * STEP_ROWS]
            )

    @pl.when(z == 0)
    def _():
        @pl.when(first)
        def _():
            moved(following.at[NX, pl.ds(0, NS - 1)], next_recv.at[2])

        @pl.when(jnp.logical_not(first))
        def _():
            moved(following.at[NX], next_recv.at[2])

        drift[0] = drift[0] + following[NX].astype(F32).reshape(STEP_ROWS, D)

    everything = drift[0] + drift[1] + drift[2] + drift[3]
    total[...] = everything.reshape(NS, PIECE, D).astype(BF16)

    def z_start(k, _):
        target = other_plane(k, z)
        pltpu.make_async_remote_copy(
            src_ref=total.at[target], dst_ref=z_in.at[z], send_sem=z_send, recv_sem=z_recv,
            device_id=to(target * NX + x, s), device_id_type=MESH,
        ).start()
        return _

    lax.fori_loop(0, NZ - 1, z_start, 0)
    z_in[z] = total[z]
    pl.when(jnp.logical_not(first))(next_all)
    moved(z_in.at[pl.ds(0, NZ - 1)], z_recv)
    running = jnp.zeros((PIECE, D), F32)
    for k in range(NZ):
        carry[k] = running.astype(BF16)
        running = running + z_in[k].astype(F32)

    def c_start(k, held):
        target = other_plane(k, z)

        @pl.when(target > 0)
        def _():
            pltpu.make_async_remote_copy(
                src_ref=carry.at[target], dst_ref=c_in.at[z], send_sem=c_send, recv_sem=c_recv,
                device_id=to(target * NX + x, s), device_id_type=MESH,
            ).start()

        return held

    lax.fori_loop(0, NZ - 1, c_start, 0)

    @pl.when(z == 0)
    def _():
        c_in[...] = jnp.zeros(c_in.shape, BF16)

    @pl.when(z > 0)
    def _():
        c_in[z] = carry[z]
        moved(c_in.at[pl.ds(0, NZ - 1)], c_recv)

    running = c_in[...].astype(F32).reshape(STEP_ROWS, D)
    for step in range(NX):
        running = running + drift[step]
        done[step] = running.reshape(NS, PIECE, D).astype(BF16)

    def u_start(k, _):
        x_to, s_to = other(k, x, s)
        pltpu.make_async_remote_copy(
            src_ref=done.at[x_to, s_to], dst_ref=out.at[own], send_sem=u_send, recv_sem=u_recv,
            device_id=to(z * NX + x_to, s_to), device_id_type=MESH,
        ).start()
        return _

    lax.fori_loop(0, NX * NS - 1, u_start, 0)
    keep = pltpu.make_async_copy(done.at[x, s], out.at[own], own_sem)
    keep.start()

    @pl.when(x == 0)
    def _():
        moved(following.at[pl.ds(0, NX - 1)], next_recv.at[0])

    @pl.when(x > 0)
    def _():
        moved(mine.at[pl.ds(0, (NX - 1) * NS - 1)], next_recv.at[0])

    @pl.when(z < NZ - 1)
    def _():
        moved(following.at[0], next_recv.at[1])

    for step in range(NX):
        difference = done[step].astype(F32) - following[step].astype(F32)
        squares = jnp.sum(difference * difference, axis=0)
        tile = squares[:, :128]
        for t in range(1, D // 128):
            tile = tile + squares[:, t * 128 : (t + 1) * 128]
        part[step] = tile

    def p_start(k, _):
        x_to, s_to = other(k, x, s)
        pltpu.make_async_remote_copy(
            src_ref=part.at[x_to], dst_ref=parts.at[x * NS + s], send_sem=p_send, recv_sem=p_recv,
            device_id=to(z * NX + x_to, s_to), device_id_type=MESH,
        ).start()
        return _

    lax.fori_loop(0, NX * NS - 1, p_start, 0)
    keep_part = pltpu.make_async_copy(part.at[x], parts.at[x * NS + s], own_part_sem)
    keep_part.start()

    moved(temper.at[pl.ds(0, NX - 1)], temper_send)
    moved(mine.at[pl.ds(0, NX * NS - 1)], y_send)

    @pl.when(plane != z)
    def _():
        moved(mine, next_send)

    @pl.when(plane == z)
    def _():
        moved(mine.at[pl.ds(0, NX * NS - 1)], next_send)

    moved(z_in.at[pl.ds(0, NZ - 1)], z_send)

    @pl.when(z == 0)
    def _():
        moved(carry.at[pl.ds(0, NZ - 1)], c_send)

    @pl.when(z > 0)
    def _():
        moved(carry.at[pl.ds(0, NZ - 2)], c_send)

    keep.wait()
    keep_part.wait()
    moved(mine.at[pl.ds(0, NX * NS - 1)], u_send)
    moved(parts.at[pl.ds(0, NX * NS - 1)], p_send)
    moved(mine.at[pl.ds(0, NX * NS - 1)], u_recv)
    moved(parts.at[pl.ds(0, NX * NS - 1)], p_recv)


def finish(rows_ref, parts_ref, out, change_ref, sem):
    copies = [
        pltpu.make_async_copy(rows_ref.at[pl.ds(i * 8, 8)], out.at[pl.ds(i * 8, 8)], sem.at[i])
        for i in range(4)
    ]
    for copy in copies:
        copy.start()
    change_ref[0] = jnp.sum(jnp.sum(parts_ref[...], axis=0)) * (1.0 / (NS * ROWS * D))
    for copy in copies:
        copy.wait()


def body(latents, timesteps, step_sizes, modulation, spatial_qkv, spatial_out, temporal_qkv, temporal_out):
    dma = pltpu.SemaphoreType.DMA

    def vmem(*shape, dtype=BF16):
        return pltpu.VMEM(shape, dtype)

    def pieces(*count):
        return pltpu.VMEM((count or (NX * NS,)) + (PIECE, D), BF16)

    table = modulation.shape[0]
    landed, parts = pl.pallas_call(
        kernel,
        out_shape=(jax.ShapeDtypeStruct((NX * NS, PIECE, D), BF16), jax.ShapeDtypeStruct((NX * NS, 8, 128), F32)),
        in_specs=[pl.BlockSpec(memory_space=pl.ANY)] * 8,
        out_specs=(pl.BlockSpec(memory_space=pl.ANY), pl.BlockSpec(memory_space=pl.ANY)),
        scratch_shapes=[
            pltpu.SMEM((1,), jnp.int32), pltpu.SMEM((1,), F32),
            pieces(), vmem(table, 6 * D),
            vmem(3 * E, D), vmem(E, D), vmem(3 * E, D), vmem(E, D),
            vmem(8, 6 * D, dtype=F32), vmem(ROWS, D),
            vmem(3 * E, ROWS, dtype=F32), vmem(2, ROWS, ROWS, dtype=F32), vmem(E, ROWS, dtype=F32),
            pieces(), pieces(), vmem(NX, 8, D, dtype=F32), pieces(NX + 1, NS),
            vmem(NX, STEP_ROWS, D, dtype=F32),
            pieces(NZ), pieces(NZ), pieces(NZ), pieces(NZ), pieces(NX, NS),
            vmem(NX, 8, 128, dtype=F32),
            dma((9,)), dma, dma, dma, dma, dma, dma((3,)),
            dma, dma, dma, dma, dma, dma, dma, dma, dma, dma,
        ],
        compiler_params=pltpu.CompilerParams(
            collective_id=0, has_side_effects=True, vmem_limit_bytes=54000 * 1024
        ),
        cost_estimate=pl.CostEstimate(
            flops=2800000000, bytes_accessed=12000000, transcendentals=1000000
        ),
    )(
        latents.reshape(NX * NS, PIECE, D), timesteps, step_sizes, modulation,
        spatial_qkv.T, spatial_out, temporal_qkv.T, temporal_out,
    )
    updated, change = pl.pallas_call(
        finish,
        out_shape=(jax.ShapeDtypeStruct(landed.shape, BF16), jax.ShapeDtypeStruct((1,), F32)),
        in_specs=[pl.BlockSpec(memory_space=pl.ANY), pl.BlockSpec(memory_space=pltpu.VMEM)],
        out_specs=(pl.BlockSpec(memory_space=pl.ANY), pl.BlockSpec(memory_space=pltpu.SMEM)),
        scratch_shapes=[dma((4,))],
    )(landed, parts)
    return updated.reshape(latents.shape), change


def solution(mesh):
    in_specs = (P("step", "seq", None, None), P("step"), P("step"), P(), P(), P(), P(), P())
    out_specs = (P("step", "seq", None, None), P("step"))
    return jax.shard_map(body, mesh=mesh, in_specs=in_specs, out_specs=out_specs, check_vma=False)
```

```python
import math

import jax
import jax.numpy as jnp
from jax import lax
from jax.experimental import pallas as pl
from jax.experimental.pallas import tpu as pltpu
from jax.sharding import PartitionSpec as P

UNROLL = 7
PROJECT = 864
MESH = pl.DeviceIdType.MESH
F32 = jnp.float32
BF16 = jnp.bfloat16

D = 1152
HEADS = 8
HEAD_DIM = 72
E = HEADS * HEAD_DIM
ROWS = 256
HALF = 128
PIECE = 8
NX = 4
NZ = 8
NS = 8
STEP_ROWS = NS * PIECE
EPS = 1e-6
LOG2E = 1.4426950408889634
Q_SCALE = 3.0 / math.sqrt(HEAD_DIM) * LOG2E


NEAR_LAST = [
    (2, 2), (2, 1), (2, 3), (1, 2), (3, 2), (1, 1), (3, 3), (1, 3),
    (3, 1), (2, 0), (0, 2), (1, 0), (0, 1), (3, 0), (0, 3), (0, 0),
]
X_OFFSETS = sum(dx << (2 * j) for j, (dx, _) in enumerate(NEAR_LAST))
Y_OFFSETS = sum(dy << (2 * j) for j, (_, dy) in enumerate(NEAR_LAST))


def chip(j, x, y):
    dx = lax.rem(lax.shift_right_logical(jnp.int32(X_OFFSETS), 2 * j), 4)
    dy = lax.rem(lax.shift_right_logical(jnp.int32(Y_OFFSETS), 2 * j), 4)
    return lax.rem(x + dx, 4), lax.rem(y + dy, 4)


def other(j, x, s):
    x_to, y_to = chip(j // 2, x, s // 2)
    return x_to, y_to * 2 + lax.rem(s + 1 + lax.rem(j, 2), 2)


def other_plane(j, z):
    return lax.rem(z + NZ // 2 + (1 - 2 * lax.rem(j, 2)) * ((j + 1) // 2), NZ)


def layer_norm(values):
    center = values - jnp.mean(values, axis=-1, keepdims=True)
    spread = jnp.mean(center * center, axis=-1, keepdims=True)
    return center * lax.rsqrt(spread + EPS)


def attend(raw, heads, scores, blocks, mask):
    def unit(start, scale):
        values = raw[pl.ds(pl.multiple_of(start, 8), HEAD_DIM), :]
        squares = jnp.sum(values * values, axis=0, keepdims=True)
        return values * (lax.rsqrt(squares * (1.0 / HEAD_DIM) + EPS) * scale)

    def ask(head):
        asked = unit(head * HEAD_DIM, Q_SCALE).astype(BF16)
        keys = unit(E + head * HEAD_DIM, 1.0).T.astype(BF16)
        for at in blocks:
            scores[lax.rem(head, 2), at, : at.stop - at.start] = jnp.dot(
                keys[at, :], asked[:, at], preferred_element_type=F32
            )

    def answer(head):
        values = raw[pl.ds(pl.multiple_of(2 * E + head * HEAD_DIM, 8), HEAD_DIM), :].astype(BF16)
        for at in blocks:
            weights = jnp.exp2(scores[lax.rem(head, 2), at, : at.stop - at.start])
            if mask is not None:
                weights = jnp.where(mask, weights, 0.0)
            inverse = 1.0 / jnp.sum(weights, axis=0, keepdims=True)
            mixed = jnp.dot(values[:, at], weights.astype(BF16), preferred_element_type=F32)
            heads[pl.ds(pl.multiple_of(head * HEAD_DIM, 8), HEAD_DIM), at] = mixed * inverse

    def one_head(head, _):
        ask(head + 1)
        answer(head)
        return _

    ask(0)
    lax.fori_loop(0, HEADS - 1, one_head, 0, unroll=UNROLL)
    answer(HEADS - 1)


def kernel(
    lat_hbm, time_hbm, size_hbm, mod_hbm, w1_hbm, o1_hbm, w2_hbm, o2_hbm,
    out, parts,
    time_ref, size_ref, lat, mod, w1, o1, w2, o2, cond, inputs, raw, scores, heads,
    after, mine, temper, state, drift, total, z_in, carry, c_in, done, part,
    local_sem, temper_send, temper_recv, y_send, y_recv, next_send, next_recv, forward_send, forward_recv,
    z_send, z_recv, c_send, c_recv, u_send, u_recv, p_send, p_recv, own_sem, own_part_sem,
):
    me = lax.axis_index("step")
    s = lax.axis_index("seq")
    z, x = me // NX, lax.rem(me, NX)

    loads = [
        pltpu.make_async_copy(src, dst, local_sem.at[i])
        for i, (src, dst) in enumerate(
            [
                (mod_hbm, mod), (lat_hbm, lat), (w1_hbm.at[pl.ds(0, PROJECT)], w1.at[pl.ds(0, PROJECT)]), (o1_hbm, o1), (w2_hbm, w2), (o2_hbm, o2),
                (time_hbm, time_ref), (size_hbm, size_ref),
                (w1_hbm.at[pl.ds(PROJECT, PROJECT)], w1.at[pl.ds(PROJECT, PROJECT)]),
            ]
        )
    ]
    for i in (6, 7, 0, 1, 2, 8, 3, 4, 5):
        loads[i].start()

    def to(step, seq):
        return {"step": step, "seq": seq}

    def greet(step, seq):
        pl.semaphore_signal(barrier, inc=1, device_id=to(step, seq), device_id_type=MESH)

    barrier = pltpu.get_barrier_semaphore()

    def greet_plane(k, _):
        greet(z * NX + lax.rem(x + k // NS, NX), lax.rem(s + lax.rem(k, NS), NS))
        return _

    lax.fori_loop(1, NX * NS, greet_plane, 0)

    def greet_planes(k, _):
        greet(lax.rem(z + k, NZ) * NX + x, s)
        return _

    lax.fori_loop(1, NZ, greet_planes, 0)

    loads[6].wait()
    loads[7].wait()
    loads[0].wait()
    one_hot = (lax.broadcasted_iota(jnp.int32, (16, mod.shape[0]), 1) == time_ref[0]).astype(BF16)
    cond[...] = jnp.dot(one_hot, mod[...], preferred_element_type=F32)[:8]

    def vector(i):
        return cond[0:1, i * D : (i + 1) * D]

    temper[x] = jnp.concatenate(
        [vector(3), 1.0 + vector(4), vector(5) * size_ref[0], jnp.broadcast_to(size_ref[0], (5, D))], axis=0
    )

    def moved(ref, sem):
        pltpu.make_async_copy(ref, ref, sem).wait()

    def normal_in(src, i, shift, scale, pieces):
        rows = pl.ds(pl.multiple_of(i * pieces * PIECE, pieces * PIECE), pieces * PIECE)
        values = src[pl.ds(i * pieces, pieces)].astype(F32).reshape(pieces * PIECE, D)
        inputs[rows, :] = (layer_norm(values) * scale + shift).astype(BF16)

    loads[1].wait()

    def spatial_in(i, _):
        normal_in(lat, i, vector(0), 1.0 + vector(1), 16)
        return _

    lax.fori_loop(0, 2, spatial_in, 0)

    contract_last = (((1,), (1,)), ((), ()))
    contract_first = (((0,), (0,)), ((), ()))

    def project(weights, i):
        rows = pl.ds(pl.multiple_of(i * PROJECT, 16), PROJECT)
        raw[rows, :] = lax.dot_general(
            weights[rows, :], inputs[...], contract_last, preferred_element_type=F32
        )

    def first_project(i, _):
        @pl.when(i == 0)
        def _():
            loads[2].wait()

        @pl.when(i == 1)
        def _():
            loads[8].wait()

        project(w1, i)
        return i

    lax.fori_loop(0, 3 * E // PROJECT, first_project, 0)
    attend(raw, heads, scores, (slice(0, ROWS),), None)
    loads[3].wait()

    pl.semaphore_wait(barrier, NX * NS - 1 + NZ - 1)

    def place(x_at, s_at):
        return lax.rem(s_at, 2) * 16 + (s_at // 2) * 4 + x_at

    own = place(x, s)

    def next_start(k, _):
        x_to, s_to = other(k, x, s)
        pltpu.make_async_remote_copy(
            src_ref=lat.at[place(x_to, s_to)], dst_ref=state.at[x, s], send_sem=next_send, recv_sem=next_recv,
            device_id=to(z * NX + x_to, s_to), device_id_type=MESH,
        ).start()
        return _

    def next_all():
        lax.fori_loop(0, NX * NS - 1, next_start, 0)
        state[x, s] = lat[own]

    def next_wait():
        moved(mine.at[pl.ds(0, NX * NS - 1)], next_recv)

    def forward():
        @pl.when(z > 0)
        def _():
            pltpu.make_async_remote_copy(
                src_ref=state.at[0], dst_ref=state.at[NX], send_sem=forward_send, recv_sem=forward_recv,
                device_id=to(me - NX, s), device_id_type=MESH,
            ).start()

    for k in range(1, NX):
        pltpu.make_async_remote_copy(
            src_ref=temper.at[x], dst_ref=temper.at[x], send_sem=temper_send, recv_sem=temper_recv,
            device_id=to(z * NX + lax.rem(x + k, NX), s), device_id_type=MESH,
        ).start()

    for half in range(2):
        rows = slice(half * HALF, (half + 1) * HALF)
        pieces = slice(half * 16, (half + 1) * 16)
        shown = lax.dot_general(
            heads[:, rows].astype(BF16), o1[...], contract_first, preferred_element_type=F32
        )
        latent = lat[pieces].astype(F32).reshape(HALF, D)
        after[pieces] = (latent + vector(2) * shown).reshape(16, PIECE, D).astype(BF16)

        def y_start(k, _):
            x_to, y_to = chip(k, x, s // 2)
            s_to = y_to * 2 + half

            @pl.when(jnp.logical_or(x_to != x, s_to != s))
            def _():
                pltpu.make_async_remote_copy(
                    src_ref=after.at[place(x_to, s_to)], dst_ref=mine.at[x * NS + s],
                    send_sem=y_send, recv_sem=y_recv,
                    device_id=to(z * NX + x_to, s_to), device_id_type=MESH,
                ).start()

            return k

        lax.fori_loop(0, 16, y_start, 0)
    mine[x * NS + s] = after[own]
    next_all()

    loads[4].wait()
    loads[5].wait()
    moved(temper.at[pl.ds(0, NX - 1)], temper_recv)
    moved(mine.at[pl.ds(0, NX * NS - 1)], y_recv)

    def temporal_in(i, _):
        normal_in(mine, i, temper[i, 0:1, :], temper[i, 1:2, :], NS)
        return _

    lax.fori_loop(0, NX, temporal_in, 0, unroll=2)

    def second_project(i, _):
        project(w2, i)
        return _

    lax.fori_loop(0, 3 * E // PROJECT, second_project, 0)
    row = lax.broadcasted_iota(jnp.int32, (HALF, HALF), 0)
    col = lax.broadcasted_iota(jnp.int32, (HALF, HALF), 1)
    same = jnp.logical_and(row // STEP_ROWS == col // STEP_ROWS, lax.rem(row, PIECE) == lax.rem(col, PIECE))
    attend(raw, heads, scores, (slice(0, HALF), slice(HALF, ROWS)), same)
    for half in range(2):
        rows = slice(half * HALF, (half + 1) * HALF)
        shown = lax.dot_general(
            heads[:, rows].astype(BF16), o2[...], contract_first, preferred_element_type=F32
        )
        for i in range(2):
            step = half * 2 + i
            rows_in = mine[step * NS : (step + 1) * NS].astype(F32).reshape(STEP_ROWS, D)
            drift[step] = (
                rows_in * temper[step, 3:4, :]
                + temper[step, 2:3, :] * shown[i * STEP_ROWS : (i + 1) * STEP_ROWS]
            )

    @pl.when(z == 0)
    def _():
        next_wait()
        drift[0] = drift[0] + state[0].astype(F32).reshape(STEP_ROWS, D)

    everything = drift[0] + drift[1] + drift[2] + drift[3]
    total[...] = everything.reshape(NS, PIECE, D).astype(BF16)

    def z_start(k, _):
        target = other_plane(k, z)
        pltpu.make_async_remote_copy(
            src_ref=total.at[target], dst_ref=z_in.at[z], send_sem=z_send, recv_sem=z_recv,
            device_id=to(target * NX + x, s), device_id_type=MESH,
        ).start()
        return _

    lax.fori_loop(0, NZ - 1, z_start, 0)
    z_in[z] = total[z]
    moved(z_in.at[pl.ds(0, NZ - 1)], z_recv)
    running = jnp.zeros((PIECE, D), F32)
    for k in range(NZ):
        carry[k] = running.astype(BF16)
        running = running + z_in[k].astype(F32)

    def c_start(k, held):
        target = other_plane(k, z)

        @pl.when(target > 0)
        def _():
            pltpu.make_async_remote_copy(
                src_ref=carry.at[target], dst_ref=c_in.at[z], send_sem=c_send, recv_sem=c_recv,
                device_id=to(target * NX + x, s), device_id_type=MESH,
            ).start()

        return held

    lax.fori_loop(0, NZ - 1, c_start, 0)
    pl.when(z > 0)(next_wait)
    forward()

    @pl.when(z == 0)
    def _():
        c_in[...] = jnp.zeros(c_in.shape, BF16)

    @pl.when(z > 0)
    def _():
        c_in[z] = carry[z]
        moved(c_in.at[pl.ds(0, NZ - 1)], c_recv)

    running = c_in[...].astype(F32).reshape(STEP_ROWS, D)
    for step in range(NX):
        running = running + drift[step]
        done[step] = running.reshape(NS, PIECE, D).astype(BF16)

    def u_start(k, _):
        x_to, s_to = other(k, x, s)
        pltpu.make_async_remote_copy(
            src_ref=done.at[x_to, s_to], dst_ref=out.at[own], send_sem=u_send, recv_sem=u_recv,
            device_id=to(z * NX + x_to, s_to), device_id_type=MESH,
        ).start()
        return _

    lax.fori_loop(0, NX * NS - 1, u_start, 0)
    keep = pltpu.make_async_copy(done.at[x, s], out.at[own], own_sem)
    keep.start()

    @pl.when(z < NZ - 1)
    def _():
        moved(state.at[NX], forward_recv)

    @pl.when(z == NZ - 1)
    def _():
        state[NX] = jnp.zeros(state.shape[1:], BF16)

    for step in range(NX):
        difference = done[step].astype(F32) - state[step + 1].astype(F32)
        squares = jnp.sum(difference * difference, axis=0)
        tile = squares[:, :128]
        for t in range(1, D // 128):
            tile = tile + squares[:, t * 128 : (t + 1) * 128]
        part[step] = tile

    def p_start(k, _):
        x_to, s_to = other(k, x, s)
        pltpu.make_async_remote_copy(
            src_ref=part.at[x_to], dst_ref=parts.at[x * NS + s], send_sem=p_send, recv_sem=p_recv,
            device_id=to(z * NX + x_to, s_to), device_id_type=MESH,
        ).start()
        return _

    lax.fori_loop(0, NX * NS - 1, p_start, 0)
    keep_part = pltpu.make_async_copy(part.at[x], parts.at[x * NS + s], own_part_sem)
    keep_part.start()

    moved(temper.at[pl.ds(0, NX - 1)], temper_send)
    moved(mine.at[pl.ds(0, NX * NS - 1)], y_send)

    moved(mine.at[pl.ds(0, NX * NS - 1)], next_send)

    @pl.when(z > 0)
    def _():
        moved(state.at[0], forward_send)

    moved(z_in.at[pl.ds(0, NZ - 1)], z_send)

    @pl.when(z == 0)
    def _():
        moved(carry.at[pl.ds(0, NZ - 1)], c_send)

    @pl.when(z > 0)
    def _():
        moved(carry.at[pl.ds(0, NZ - 2)], c_send)

    keep.wait()
    keep_part.wait()
    moved(mine.at[pl.ds(0, NX * NS - 1)], u_send)
    moved(parts.at[pl.ds(0, NX * NS - 1)], p_send)
    moved(mine.at[pl.ds(0, NX * NS - 1)], u_recv)
    moved(parts.at[pl.ds(0, NX * NS - 1)], p_recv)


def finish(rows_ref, parts_ref, out, change_ref, sem):
    copies = [
        pltpu.make_async_copy(rows_ref.at[pl.ds(i * 8, 8)], out.at[pl.ds(i * 8, 8)], sem.at[i])
        for i in range(4)
    ]
    for copy in copies:
        copy.start()
    change_ref[0] = jnp.sum(jnp.sum(parts_ref[...], axis=0)) * (1.0 / (NS * ROWS * D))
    for copy in copies:
        copy.wait()


def body(latents, timesteps, step_sizes, modulation, spatial_qkv, spatial_out, temporal_qkv, temporal_out):
    dma = pltpu.SemaphoreType.DMA

    def vmem(*shape, dtype=BF16):
        return pltpu.VMEM(shape, dtype)

    def pieces(*count):
        return pltpu.VMEM((count or (NX * NS,)) + (PIECE, D), BF16)

    table = modulation.shape[0]
    landed, parts = pl.pallas_call(
        kernel,
        out_shape=(jax.ShapeDtypeStruct((NX * NS, PIECE, D), BF16), jax.ShapeDtypeStruct((NX * NS, 8, 128), F32)),
        in_specs=[pl.BlockSpec(memory_space=pl.ANY)] * 8,
        out_specs=(pl.BlockSpec(memory_space=pl.ANY), pl.BlockSpec(memory_space=pl.ANY)),
        scratch_shapes=[
            pltpu.SMEM((1,), jnp.int32), pltpu.SMEM((1,), F32),
            pieces(), vmem(table, 6 * D),
            vmem(3 * E, D), vmem(E, D), vmem(3 * E, D), vmem(E, D),
            vmem(8, 6 * D, dtype=F32), vmem(ROWS, D),
            vmem(3 * E, ROWS, dtype=F32), vmem(2, ROWS, ROWS, dtype=F32), vmem(E, ROWS, dtype=F32),
            pieces(), pieces(), vmem(NX, 8, D, dtype=F32), pieces(NX + 1, NS),
            vmem(NX, STEP_ROWS, D, dtype=F32),
            pieces(NZ), pieces(NZ), pieces(NZ), pieces(NZ), pieces(NX, NS),
            vmem(NX, 8, 128, dtype=F32),
            dma((9,)), dma, dma, dma, dma, dma, dma, dma, dma,
            dma, dma, dma, dma, dma, dma, dma, dma, dma, dma,
        ],
        compiler_params=pltpu.CompilerParams(
            collective_id=0, has_side_effects=True, vmem_limit_bytes=54000 * 1024
        ),
        cost_estimate=pl.CostEstimate(
            flops=2800000000, bytes_accessed=12000000, transcendentals=1000000
        ),
    )(
        latents.reshape(NX * NS, PIECE, D), timesteps, step_sizes, modulation,
        spatial_qkv.T, spatial_out, temporal_qkv.T, temporal_out,
    )
    updated, change = pl.pallas_call(
        finish,
        out_shape=(jax.ShapeDtypeStruct(landed.shape, BF16), jax.ShapeDtypeStruct((1,), F32)),
        in_specs=[pl.BlockSpec(memory_space=pl.ANY), pl.BlockSpec(memory_space=pltpu.VMEM)],
        out_specs=(pl.BlockSpec(memory_space=pl.ANY), pl.BlockSpec(memory_space=pltpu.SMEM)),
        scratch_shapes=[dma((4,))],
        compiler_params=pltpu.CompilerParams(vmem_limit_bytes=4 * 1024 * 1024),
    )(landed, parts)
    return updated.reshape(latents.shape), change


def solution(mesh):
    in_specs = (P("step", "seq", None, None), P("step"), P("step"), P(), P(), P(), P(), P())
    out_specs = (P("step", "seq", None, None), P("step"))
    return jax.shard_map(body, mesh=mesh, in_specs=in_specs, out_specs=out_specs, check_vma=False)
```

```python
import math

import jax
import jax.numpy as jnp
from jax import lax
from jax.experimental import pallas as pl
from jax.experimental.pallas import tpu as pltpu
from jax.sharding import PartitionSpec as P

UNROLL = 7
PROJECT = 864
MESH = pl.DeviceIdType.MESH
F32 = jnp.float32
BF16 = jnp.bfloat16

D = 1152
HEADS = 8
HEAD_DIM = 72
E = HEADS * HEAD_DIM
ROWS = 256
HALF = 128
PIECE = 8
NX = 4
NZ = 8
NS = 8
STEP_ROWS = NS * PIECE
EPS = 1e-6
LOG2E = 1.4426950408889634
Q_SCALE = 3.0 / math.sqrt(HEAD_DIM) * LOG2E


NEAR_LAST = [
    (2, 2), (2, 1), (2, 3), (1, 2), (3, 2), (1, 1), (3, 3), (1, 3),
    (3, 1), (2, 0), (0, 2), (1, 0), (0, 1), (3, 0), (0, 3), (0, 0),
]
X_OFFSETS = sum(dx << (2 * j) for j, (dx, _) in enumerate(NEAR_LAST))
Y_OFFSETS = sum(dy << (2 * j) for j, (_, dy) in enumerate(NEAR_LAST))


def chip(j, x, y):
    dx = lax.rem(lax.shift_right_logical(jnp.int32(X_OFFSETS), 2 * j), 4)
    dy = lax.rem(lax.shift_right_logical(jnp.int32(Y_OFFSETS), 2 * j), 4)
    return lax.rem(x + dx, 4), lax.rem(y + dy, 4)


def other(j, x, s):
    x_to, y_to = chip(j // 2, x, s // 2)
    return x_to, y_to * 2 + lax.rem(s + 1 + lax.rem(j, 2), 2)


def other_plane(j, z):
    return lax.rem(z + NZ // 2 + (1 - 2 * lax.rem(j, 2)) * ((j + 1) // 2), NZ)


def layer_norm(values):
    center = values - jnp.mean(values, axis=-1, keepdims=True)
    spread = jnp.mean(center * center, axis=-1, keepdims=True)
    return center * lax.rsqrt(spread + EPS)


def attend(raw, heads, scores, blocks, mask):
    def unit(start, scale):
        values = raw[pl.ds(pl.multiple_of(start, 8), HEAD_DIM), :]
        squares = jnp.sum(values * values, axis=0, keepdims=True)
        return values * (lax.rsqrt(squares * (1.0 / HEAD_DIM) + EPS) * scale)

    def ask(head):
        asked = unit(head * HEAD_DIM, Q_SCALE).astype(BF16)
        keys = unit(E + head * HEAD_DIM, 1.0).T.astype(BF16)
        for at in blocks:
            scores[lax.rem(head, 2), at, : at.stop - at.start] = jnp.dot(
                keys[at, :], asked[:, at], preferred_element_type=F32
            )

    def answer(head):
        values = raw[pl.ds(pl.multiple_of(2 * E + head * HEAD_DIM, 8), HEAD_DIM), :].astype(BF16)
        for at in blocks:
            weights = jnp.exp2(scores[lax.rem(head, 2), at, : at.stop - at.start])
            if mask is not None:
                weights = jnp.where(mask, weights, 0.0)
            inverse = 1.0 / jnp.sum(weights, axis=0, keepdims=True)
            mixed = jnp.dot(values[:, at], weights.astype(BF16), preferred_element_type=F32)
            heads[pl.ds(pl.multiple_of(head * HEAD_DIM, 8), HEAD_DIM), at] = mixed * inverse

    def one_head(head, _):
        ask(head + 1)
        answer(head)
        return _

    ask(0)
    lax.fori_loop(0, HEADS - 1, one_head, 0, unroll=UNROLL)
    answer(HEADS - 1)


def kernel(
    lat_hbm, time_hbm, size_hbm, mod_hbm, w1_hbm, o1_hbm, w2_hbm, o2_hbm,
    out_a, out_b, parts,
    time_ref, size_ref, lat, mod, w1, o1, w2, o2, cond, inputs, raw, scores, heads,
    after, mine, temper, state, drift, total, z_in, carry, c_in, done, part,
    local_sem, temper_send, temper_recv, y_send, y_recv, next_send, next_recv, forward_send, forward_recv,
    z_send, z_recv, c_send, c_recv, u_send, u_recv, p_send, p_recv, own_sem, own_part_sem,
):
    me = lax.axis_index("step")
    s = lax.axis_index("seq")
    z, x = me // NX, lax.rem(me, NX)

    loads = [
        pltpu.make_async_copy(src, dst, local_sem.at[i])
        for i, (src, dst) in enumerate(
            [
                (mod_hbm, mod), (lat_hbm, lat), (w1_hbm.at[pl.ds(0, PROJECT)], w1.at[pl.ds(0, PROJECT)]), (o1_hbm, o1), (w2_hbm, w2), (o2_hbm, o2),
                (time_hbm, time_ref), (size_hbm, size_ref),
                (w1_hbm.at[pl.ds(PROJECT, PROJECT)], w1.at[pl.ds(PROJECT, PROJECT)]),
            ]
        )
    ]
    for i in (6, 7, 0, 1, 2, 8, 3, 4, 5):
        loads[i].start()

    def to(step, seq):
        return {"step": step, "seq": seq}

    def greet(step, seq):
        pl.semaphore_signal(barrier, inc=1, device_id=to(step, seq), device_id_type=MESH)

    barrier = pltpu.get_barrier_semaphore()

    def greet_plane(k, _):
        greet(z * NX + lax.rem(x + k // NS, NX), lax.rem(s + lax.rem(k, NS), NS))
        return _

    lax.fori_loop(1, NX * NS, greet_plane, 0)

    def greet_planes(k, _):
        greet(lax.rem(z + k, NZ) * NX + x, s)
        return _

    lax.fori_loop(1, NZ, greet_planes, 0)

    loads[6].wait()
    loads[7].wait()
    loads[0].wait()
    one_hot = (lax.broadcasted_iota(jnp.int32, (16, mod.shape[0]), 1) == time_ref[0]).astype(BF16)
    cond[...] = jnp.dot(one_hot, mod[...], preferred_element_type=F32)[:8]

    def vector(i):
        return cond[0:1, i * D : (i + 1) * D]

    temper[x] = jnp.concatenate(
        [vector(3), 1.0 + vector(4), vector(5) * size_ref[0], jnp.broadcast_to(size_ref[0], (5, D))], axis=0
    )

    def moved(ref, sem):
        pltpu.make_async_copy(ref, ref, sem).wait()

    def normal_in(src, i, shift, scale, pieces):
        rows = pl.ds(pl.multiple_of(i * pieces * PIECE, pieces * PIECE), pieces * PIECE)
        values = src[pl.ds(i * pieces, pieces)].astype(F32).reshape(pieces * PIECE, D)
        inputs[rows, :] = (layer_norm(values) * scale + shift).astype(BF16)

    loads[1].wait()

    def spatial_in(i, _):
        normal_in(lat, i, vector(0), 1.0 + vector(1), 16)
        return _

    lax.fori_loop(0, 2, spatial_in, 0)

    contract_last = (((1,), (1,)), ((), ()))
    contract_first = (((0,), (0,)), ((), ()))

    def project(weights, i):
        rows = pl.ds(pl.multiple_of(i * PROJECT, 16), PROJECT)
        raw[rows, :] = lax.dot_general(
            weights[rows, :], inputs[...], contract_last, preferred_element_type=F32
        )

    def first_project(i, _):
        @pl.when(i == 0)
        def _():
            loads[2].wait()

        @pl.when(i == 1)
        def _():
            loads[8].wait()

        project(w1, i)
        return i

    lax.fori_loop(0, 3 * E // PROJECT, first_project, 0)
    attend(raw, heads, scores, (slice(0, ROWS),), None)
    loads[3].wait()

    pl.semaphore_wait(barrier, NX * NS - 1 + NZ - 1)

    def place(x_at, s_at):
        return lax.rem(s_at, 2) * 16 + (s_at // 2) * 4 + x_at

    own = place(x, s)

    def next_start(k, _):
        x_to, s_to = other(k, x, s)
        pltpu.make_async_remote_copy(
            src_ref=lat.at[place(x_to, s_to)], dst_ref=state.at[x, s], send_sem=next_send, recv_sem=next_recv,
            device_id=to(z * NX + x_to, s_to), device_id_type=MESH,
        ).start()
        return _

    def next_all():
        lax.fori_loop(0, NX * NS - 1, next_start, 0)
        state[x, s] = lat[own]

    def next_wait():
        moved(mine.at[pl.ds(0, NX * NS - 1)], next_recv)

    def forward():
        @pl.when(z > 0)
        def _():
            pltpu.make_async_remote_copy(
                src_ref=state.at[0], dst_ref=state.at[NX], send_sem=forward_send, recv_sem=forward_recv,
                device_id=to(me - NX, s), device_id_type=MESH,
            ).start()

    for k in range(1, NX):
        pltpu.make_async_remote_copy(
            src_ref=temper.at[x], dst_ref=temper.at[x], send_sem=temper_send, recv_sem=temper_recv,
            device_id=to(z * NX + lax.rem(x + k, NX), s), device_id_type=MESH,
        ).start()

    for half in range(2):
        rows = slice(half * HALF, (half + 1) * HALF)
        pieces = slice(half * 16, (half + 1) * 16)
        shown = lax.dot_general(
            heads[:, rows].astype(BF16), o1[...], contract_first, preferred_element_type=F32
        )
        latent = lat[pieces].astype(F32).reshape(HALF, D)
        after[pieces] = (latent + vector(2) * shown).reshape(16, PIECE, D).astype(BF16)

        def y_start(k, _):
            x_to, y_to = chip(k, x, s // 2)
            s_to = y_to * 2 + half

            @pl.when(jnp.logical_or(x_to != x, s_to != s))
            def _():
                pltpu.make_async_remote_copy(
                    src_ref=after.at[place(x_to, s_to)], dst_ref=mine.at[x * NS + s],
                    send_sem=y_send, recv_sem=y_recv,
                    device_id=to(z * NX + x_to, s_to), device_id_type=MESH,
                ).start()

            return k

        lax.fori_loop(0, 16, y_start, 0)
    mine[x * NS + s] = after[own]
    next_all()

    loads[4].wait()
    loads[5].wait()
    moved(temper.at[pl.ds(0, NX - 1)], temper_recv)
    moved(mine.at[pl.ds(0, NX * NS - 1)], y_recv)

    def temporal_in(i, _):
        normal_in(mine, i, temper[i, 0:1, :], temper[i, 1:2, :], NS)
        return _

    lax.fori_loop(0, NX, temporal_in, 0, unroll=2)

    def second_project(i, _):
        project(w2, i)
        return _

    lax.fori_loop(0, 3 * E // PROJECT, second_project, 0)
    row = lax.broadcasted_iota(jnp.int32, (HALF, HALF), 0)
    col = lax.broadcasted_iota(jnp.int32, (HALF, HALF), 1)
    same = jnp.logical_and(row // STEP_ROWS == col // STEP_ROWS, lax.rem(row, PIECE) == lax.rem(col, PIECE))
    attend(raw, heads, scores, (slice(0, HALF), slice(HALF, ROWS)), same)
    for half in range(2):
        rows = slice(half * HALF, (half + 1) * HALF)
        shown = lax.dot_general(
            heads[:, rows].astype(BF16), o2[...], contract_first, preferred_element_type=F32
        )
        for i in range(2):
            step = half * 2 + i
            rows_in = mine[step * NS : (step + 1) * NS].astype(F32).reshape(STEP_ROWS, D)
            drift[step] = (
                rows_in * temper[step, 3:4, :]
                + temper[step, 2:3, :] * shown[i * STEP_ROWS : (i + 1) * STEP_ROWS]
            )

    @pl.when(z == 0)
    def _():
        next_wait()
        drift[0] = drift[0] + state[0].astype(F32).reshape(STEP_ROWS, D)

    everything = drift[0] + drift[1] + drift[2] + drift[3]
    total[...] = everything.reshape(NS, PIECE, D).astype(BF16)

    def z_start(k, _):
        target = other_plane(k, z)
        pltpu.make_async_remote_copy(
            src_ref=total.at[target], dst_ref=z_in.at[z], send_sem=z_send, recv_sem=z_recv.at[z],
            device_id=to(target * NX + x, s), device_id_type=MESH,
        ).start()
        return _

    @pl.when(z < NZ - 1)
    def _():
        lax.fori_loop(0, NZ - 1, z_start, 0)
        z_in[z] = total[z]

    running = jnp.zeros((PIECE, D), F32)
    for k in range(NZ - 1):

        @pl.when(z != k)
        def _():
            moved(z_in.at[k], z_recv.at[k])

        running = running + z_in[k].astype(F32)
        carry[k + 1] = running.astype(BF16)

        @pl.when(z != k + 1)
        def _():
            pltpu.make_async_remote_copy(
                src_ref=carry.at[k + 1], dst_ref=c_in.at[z], send_sem=c_send, recv_sem=c_recv,
                device_id=to((k + 1) * NX + x, s), device_id_type=MESH,
            ).start()

    pl.when(z > 0)(next_wait)
    forward()

    @pl.when(z == 0)
    def _():
        c_in[...] = jnp.zeros(c_in.shape, BF16)

    @pl.when(z > 0)
    def _():
        c_in[z] = carry[z]
        moved(c_in.at[pl.ds(0, NZ - 1)], c_recv)

    running = c_in[...].astype(F32).reshape(STEP_ROWS, D)
    for step in range(NX):
        running = running + drift[step]
        done[step] = running.reshape(NS, PIECE, D).astype(BF16)

    def rows_out(out, at):
        def u_start(k, _):
            x_to, s_to = other(k, x, s)
            pltpu.make_async_remote_copy(
                src_ref=done.at[x_to, s_to], dst_ref=out.at[at], send_sem=u_send, recv_sem=u_recv,
                device_id=to(z * NX + x_to, s_to), device_id_type=MESH,
            ).start()
            return _

        lax.fori_loop(0, NX * NS - 1, u_start, 0)
        pltpu.make_async_copy(done.at[x, s], out.at[at], own_sem).start()

    at = lax.rem(own, 16)

    @pl.when(lax.rem(s, 2) == 0)
    def _():
        rows_out(out_a, at)

    @pl.when(lax.rem(s, 2) == 1)
    def _():
        rows_out(out_b, at)

    @pl.when(z < NZ - 1)
    def _():
        moved(state.at[NX], forward_recv)

    @pl.when(z == NZ - 1)
    def _():
        state[NX] = jnp.zeros(state.shape[1:], BF16)

    for step in range(NX):
        difference = done[step].astype(F32) - state[step + 1].astype(F32)
        squares = jnp.sum(difference * difference, axis=0)
        tile = squares[:, :128]
        for t in range(1, D // 128):
            tile = tile + squares[:, t * 128 : (t + 1) * 128]
        part[step] = tile

    def p_start(k, _):
        x_to, s_to = other(k, x, s)
        pltpu.make_async_remote_copy(
            src_ref=part.at[x_to], dst_ref=parts.at[x * NS + s], send_sem=p_send, recv_sem=p_recv,
            device_id=to(z * NX + x_to, s_to), device_id_type=MESH,
        ).start()
        return _

    lax.fori_loop(0, NX * NS - 1, p_start, 0)
    keep_part = pltpu.make_async_copy(part.at[x], parts.at[x * NS + s], own_part_sem)
    keep_part.start()

    moved(temper.at[pl.ds(0, NX - 1)], temper_send)
    moved(mine.at[pl.ds(0, NX * NS - 1)], y_send)

    moved(mine.at[pl.ds(0, NX * NS - 1)], next_send)

    @pl.when(z > 0)
    def _():
        moved(state.at[0], forward_send)


    @pl.when(z < NZ - 1)
    def _():
        moved(z_in.at[pl.ds(0, NZ - 1)], z_send)

    @pl.when(z == 0)
    def _():
        moved(carry.at[pl.ds(0, NZ - 1)], c_send)

    @pl.when(z > 0)
    def _():
        moved(carry.at[pl.ds(0, NZ - 2)], c_send)

    moved(mine.at[0], own_sem)
    keep_part.wait()
    moved(mine.at[pl.ds(0, NX * NS - 1)], u_send)
    moved(parts.at[pl.ds(0, NX * NS - 1)], p_send)
    moved(mine.at[pl.ds(0, NX * NS - 1)], u_recv)
    moved(parts.at[pl.ds(0, NX * NS - 1)], p_recv)


def finish(first_ref, second_ref, parts_ref, out, change_ref, sem):
    copies = [
        pltpu.make_async_copy(ref, out.at[pl.ds(i * 16, 16)], sem.at[i])
        for i, ref in enumerate((first_ref, second_ref))
    ]
    for copy in copies:
        copy.start()
    change_ref[0] = jnp.sum(jnp.sum(parts_ref[...], axis=0)) * (1.0 / (NS * ROWS * D))
    for copy in copies:
        copy.wait()


def body(latents, timesteps, step_sizes, modulation, spatial_qkv, spatial_out, temporal_qkv, temporal_out):
    dma = pltpu.SemaphoreType.DMA

    def vmem(*shape, dtype=BF16):
        return pltpu.VMEM(shape, dtype)

    def pieces(*count):
        return pltpu.VMEM((count or (NX * NS,)) + (PIECE, D), BF16)

    half_rows = jax.ShapeDtypeStruct((NX * NS // 2, PIECE, D), BF16)
    table = modulation.shape[0]
    first, second, parts = pl.pallas_call(
        kernel,
        out_shape=(half_rows, half_rows, jax.ShapeDtypeStruct((NX * NS, 8, 128), F32)),
        in_specs=[pl.BlockSpec(memory_space=pl.ANY)] * 8,
        out_specs=(pl.BlockSpec(memory_space=pl.ANY),) * 3,
        scratch_shapes=[
            pltpu.SMEM((1,), jnp.int32), pltpu.SMEM((1,), F32),
            pieces(), vmem(table, 6 * D),
            vmem(3 * E, D), vmem(E, D), vmem(3 * E, D), vmem(E, D),
            vmem(8, 6 * D, dtype=F32), vmem(ROWS, D),
            vmem(3 * E, ROWS, dtype=F32), vmem(2, ROWS, ROWS, dtype=F32), vmem(E, ROWS, dtype=F32),
            pieces(), pieces(), vmem(NX, 8, D, dtype=F32), pieces(NX + 1, NS),
            vmem(NX, STEP_ROWS, D, dtype=F32),
            pieces(NZ), pieces(NZ), pieces(NZ), pieces(NZ), pieces(NX, NS),
            vmem(NX, 8, 128, dtype=F32),
            dma((9,)), dma, dma, dma, dma, dma, dma, dma, dma,
            dma, dma((NZ,)), dma, dma, dma, dma, dma, dma, dma, dma,
        ],
        compiler_params=pltpu.CompilerParams(
            collective_id=0, has_side_effects=True, vmem_limit_bytes=54374 * 1024
        ),
        cost_estimate=pl.CostEstimate(
            flops=2800000000, bytes_accessed=12000000, transcendentals=1000000
        ),
    )(
        latents.reshape(NX * NS, PIECE, D), timesteps, step_sizes, modulation,
        spatial_qkv.T, spatial_out, temporal_qkv.T, temporal_out,
    )
    updated, change = pl.pallas_call(
        finish,
        out_shape=(jax.ShapeDtypeStruct((NX * NS, PIECE, D), BF16), jax.ShapeDtypeStruct((1,), F32)),
        in_specs=[pl.BlockSpec(memory_space=pl.ANY)] * 2 + [pl.BlockSpec(memory_space=pltpu.VMEM)],
        out_specs=(pl.BlockSpec(memory_space=pl.ANY), pl.BlockSpec(memory_space=pltpu.SMEM)),
        scratch_shapes=[dma((2,))],
        compiler_params=pltpu.CompilerParams(vmem_limit_bytes=4 * 1024 * 1024),
    )(first, second, parts)
    return updated.reshape(latents.shape), change


def solution(mesh):
    in_specs = (P("step", "seq", None, None), P("step"), P("step"), P(), P(), P(), P(), P())
    out_specs = (P("step", "seq", None, None), P("step"))
    return jax.shard_map(body, mesh=mesh, in_specs=in_specs, out_specs=out_specs, check_vma=False)
```

```python
import math

import jax
import jax.numpy as jnp
from jax import lax
from jax.experimental import pallas as pl
from jax.experimental.pallas import tpu as pltpu
from jax.sharding import PartitionSpec as P

UNROLL = 7
PROJECT = 864
MESH = pl.DeviceIdType.MESH
F32 = jnp.float32
BF16 = jnp.bfloat16

D = 1152
HEADS = 8
HEAD_DIM = 72
E = HEADS * HEAD_DIM
ROWS = 256
HALF = 128
PIECE = 8
NX = 4
NZ = 8
NS = 8
GROUP = 4
STEP_ROWS = NS * PIECE
EPS = 1e-6
LOG2E = 1.4426950408889634
Q_SCALE = 3.0 / math.sqrt(HEAD_DIM) * LOG2E


NEAR_LAST = [
    (2, 2), (2, 1), (2, 3), (1, 2), (3, 2), (1, 1), (3, 3), (1, 3),
    (3, 1), (2, 0), (0, 2), (1, 0), (0, 1), (3, 0), (0, 3), (0, 0),
]
X_OFFSETS = sum(dx << (2 * j) for j, (dx, _) in enumerate(NEAR_LAST))
Y_OFFSETS = sum(dy << (2 * j) for j, (_, dy) in enumerate(NEAR_LAST))


def chip(j, x, y):
    dx = lax.rem(lax.shift_right_logical(jnp.int32(X_OFFSETS), 2 * j), 4)
    dy = lax.rem(lax.shift_right_logical(jnp.int32(Y_OFFSETS), 2 * j), 4)
    return lax.rem(x + dx, 4), lax.rem(y + dy, 4)


def other(j, x, s):
    x_to, y_to = chip(j // 2, x, s // 2)
    return x_to, y_to * 2 + lax.rem(s + 1 + lax.rem(j, 2), 2)


def layer_norm(values):
    center = values - jnp.mean(values, axis=-1, keepdims=True)
    spread = jnp.mean(center * center, axis=-1, keepdims=True)
    return center * lax.rsqrt(spread + EPS)


def attend(raw, heads, scores, blocks, mask):
    def unit(start, scale):
        values = raw[pl.ds(pl.multiple_of(start, 8), HEAD_DIM), :]
        squares = jnp.sum(values * values, axis=0, keepdims=True)
        return values * (lax.rsqrt(squares * (1.0 / HEAD_DIM) + EPS) * scale)

    def ask(head):
        asked = unit(head * HEAD_DIM, Q_SCALE).astype(BF16)
        keys = unit(E + head * HEAD_DIM, 1.0).T.astype(BF16)
        for at in blocks:
            scores[lax.rem(head, 2), at, : at.stop - at.start] = jnp.dot(
                keys[at, :], asked[:, at], preferred_element_type=F32
            )

    def answer(head):
        values = raw[pl.ds(pl.multiple_of(2 * E + head * HEAD_DIM, 8), HEAD_DIM), :].astype(BF16)
        for at in blocks:
            weights = jnp.exp2(scores[lax.rem(head, 2), at, : at.stop - at.start])
            if mask is not None:
                weights = jnp.where(mask, weights, 0.0)
            inverse = 1.0 / jnp.sum(weights, axis=0, keepdims=True)
            mixed = jnp.dot(values[:, at], weights.astype(BF16), preferred_element_type=F32)
            heads[pl.ds(pl.multiple_of(head * HEAD_DIM, 8), HEAD_DIM), at] = mixed * inverse

    def one_head(head, _):
        ask(head + 1)
        answer(head)
        return _

    ask(0)
    lax.fori_loop(0, HEADS - 1, one_head, 0, unroll=UNROLL)
    answer(HEADS - 1)


def kernel(
    lat_hbm, time_hbm, size_hbm, mod_hbm, w1_hbm, o1_hbm, w2_hbm, o2_hbm,
    out_a, out_b, parts,
    time_ref, size_ref, lat, mod, w1, o1, w2, o2, cond, inputs, raw, scores, heads,
    after, mine, temper, state, drift, total, z_in, carry, c_in, done, part,
    local_sem, temper_send, temper_recv, y_send, y_recv, next_send, next_recv, forward_send, forward_recv,
    z_send, z_recv, c_send, c_recv, u_sent, u_recv, p_send, p_recv, own_sem, own_part_sem,
):
    me = lax.axis_index("step")
    s = lax.axis_index("seq")
    z, x = me // NX, lax.rem(me, NX)

    loads = [
        pltpu.make_async_copy(src, dst, local_sem.at[i])
        for i, (src, dst) in enumerate(
            [
                (mod_hbm, mod), (lat_hbm, lat), (w1_hbm.at[pl.ds(0, PROJECT)], w1.at[pl.ds(0, PROJECT)]), (o1_hbm, o1), (w2_hbm, w2), (o2_hbm, o2),
                (time_hbm, time_ref), (size_hbm, size_ref),
                (w1_hbm.at[pl.ds(PROJECT, PROJECT)], w1.at[pl.ds(PROJECT, PROJECT)]),
            ]
        )
    ]
    for i in (6, 7, 0, 1, 2, 8, 3, 4, 5):
        loads[i].start()

    def to(step, seq):
        return {"step": step, "seq": seq}

    def greet(step, seq):
        pl.semaphore_signal(barrier, inc=1, device_id=to(step, seq), device_id_type=MESH)

    barrier = pltpu.get_barrier_semaphore()

    def greet_plane(k, _):
        greet(z * NX + lax.rem(x + k // NS, NX), lax.rem(s + lax.rem(k, NS), NS))
        return _

    lax.fori_loop(1, NX * NS, greet_plane, 0)

    def greet_planes(k, _):
        greet(lax.rem(z + k, NZ) * NX + x, s)
        return _

    lax.fori_loop(1, NZ, greet_planes, 0)

    loads[6].wait()
    loads[7].wait()
    loads[0].wait()
    one_hot = (lax.broadcasted_iota(jnp.int32, (16, mod.shape[0]), 1) == time_ref[0]).astype(BF16)
    cond[...] = jnp.dot(one_hot, mod[...], preferred_element_type=F32)[:8]

    def vector(i):
        return cond[0:1, i * D : (i + 1) * D]

    temper[x] = jnp.concatenate(
        [vector(3), 1.0 + vector(4), vector(5) * size_ref[0], jnp.broadcast_to(size_ref[0], (5, D))], axis=0
    )

    def moved(ref, sem):
        pltpu.make_async_copy(ref, ref, sem).wait()

    def normal_in(src, i, shift, scale, pieces):
        rows = pl.ds(pl.multiple_of(i * pieces * PIECE, pieces * PIECE), pieces * PIECE)
        values = src[pl.ds(i * pieces, pieces)].astype(F32).reshape(pieces * PIECE, D)
        inputs[rows, :] = (layer_norm(values) * scale + shift).astype(BF16)

    loads[1].wait()

    def spatial_in(i, _):
        normal_in(lat, i, vector(0), 1.0 + vector(1), 16)
        return _

    lax.fori_loop(0, 2, spatial_in, 0)

    contract_last = (((1,), (1,)), ((), ()))
    contract_first = (((0,), (0,)), ((), ()))

    def project(weights, i):
        rows = pl.ds(pl.multiple_of(i * PROJECT, 16), PROJECT)
        raw[rows, :] = lax.dot_general(
            weights[rows, :], inputs[...], contract_last, preferred_element_type=F32
        )

    def first_project(i, _):
        @pl.when(i == 0)
        def _():
            loads[2].wait()

        @pl.when(i == 1)
        def _():
            loads[8].wait()

        project(w1, i)
        return i

    lax.fori_loop(0, 3 * E // PROJECT, first_project, 0)
    attend(raw, heads, scores, (slice(0, ROWS),), None)
    loads[3].wait()

    pl.semaphore_wait(barrier, NX * NS - 1 + NZ - 1)

    def place(x_at, s_at):
        return lax.rem(s_at, 2) * 16 + (s_at // 2) * 4 + x_at

    own = place(x, s)

    def next_start(k, _):
        x_to, s_to = other(k, x, s)
        pltpu.make_async_remote_copy(
            src_ref=lat.at[place(x_to, s_to)], dst_ref=state.at[x, s], send_sem=next_send, recv_sem=next_recv,
            device_id=to(z * NX + x_to, s_to), device_id_type=MESH,
        ).start()
        return _

    def next_all():
        lax.fori_loop(0, NX * NS - 1, next_start, 0)
        state[x, s] = lat[own]

    def next_wait():
        moved(mine.at[pl.ds(0, NX * NS - 1)], next_recv)

    def forward():
        @pl.when(z > 0)
        def _():
            pltpu.make_async_remote_copy(
                src_ref=state.at[0], dst_ref=state.at[NX], send_sem=forward_send, recv_sem=forward_recv,
                device_id=to(me - NX, s), device_id_type=MESH,
            ).start()

    for k in range(1, NX):
        pltpu.make_async_remote_copy(
            src_ref=temper.at[x], dst_ref=temper.at[x], send_sem=temper_send, recv_sem=temper_recv,
            device_id=to(z * NX + lax.rem(x + k, NX), s), device_id_type=MESH,
        ).start()

    for half in range(2):
        rows = slice(half * HALF, (half + 1) * HALF)
        pieces = slice(half * 16, (half + 1) * 16)
        shown = lax.dot_general(
            heads[:, rows].astype(BF16), o1[...], contract_first, preferred_element_type=F32
        )
        latent = lat[pieces].astype(F32).reshape(HALF, D)
        after[pieces] = (latent + vector(2) * shown).reshape(16, PIECE, D).astype(BF16)

        def y_start(k, _):
            x_to, y_to = chip(k, x, s // 2)
            s_to = y_to * 2 + half

            @pl.when(jnp.logical_or(x_to != x, s_to != s))
            def _():
                pltpu.make_async_remote_copy(
                    src_ref=after.at[place(x_to, s_to)], dst_ref=mine.at[x * NS + s],
                    send_sem=y_send, recv_sem=y_recv,
                    device_id=to(z * NX + x_to, s_to), device_id_type=MESH,
                ).start()

            return k

        lax.fori_loop(0, 16, y_start, 0)
    mine[x * NS + s] = after[own]
    next_all()

    loads[4].wait()
    loads[5].wait()
    moved(temper.at[pl.ds(0, NX - 1)], temper_recv)
    moved(mine.at[pl.ds(0, NX * NS - 1)], y_recv)

    def temporal_in(i, _):
        normal_in(mine, i, temper[i, 0:1, :], temper[i, 1:2, :], NS)
        return _

    lax.fori_loop(0, NX, temporal_in, 0, unroll=2)

    def second_project(i, _):
        project(w2, i)
        return _

    lax.fori_loop(0, 3 * E // PROJECT, second_project, 0)
    row = lax.broadcasted_iota(jnp.int32, (HALF, HALF), 0)
    col = lax.broadcasted_iota(jnp.int32, (HALF, HALF), 1)
    same = jnp.logical_and(row // STEP_ROWS == col // STEP_ROWS, lax.rem(row, PIECE) == lax.rem(col, PIECE))
    attend(raw, heads, scores, (slice(0, HALF), slice(HALF, ROWS)), same)
    for half in range(2):
        rows = slice(half * HALF, (half + 1) * HALF)
        shown = lax.dot_general(
            heads[:, rows].astype(BF16), o2[...], contract_first, preferred_element_type=F32
        )
        for i in range(2):
            step = half * 2 + i
            rows_in = mine[step * NS : (step + 1) * NS].astype(F32).reshape(STEP_ROWS, D)
            drift[step] = (
                rows_in * temper[step, 3:4, :]
                + temper[step, 2:3, :] * shown[i * STEP_ROWS : (i + 1) * STEP_ROWS]
            )

    @pl.when(z == 0)
    def _():
        next_wait()
        drift[0] = drift[0] + state[0].astype(F32).reshape(STEP_ROWS, D)

    everything = drift[0] + drift[1] + drift[2] + drift[3]
    total[...] = everything.reshape(NS, PIECE, D).astype(BF16)

    def pair(holder):
        return lax.rem(holder + x + s // 2, GROUP)

    def z_send_to(target):
        pltpu.make_async_remote_copy(
            src_ref=total.at[pl.ds(2 * pair(target % GROUP), 2)], dst_ref=z_in.at[z],
            send_sem=z_send, recv_sem=z_recv.at[z],
            device_id=to(target * NX + x, s), device_id_type=MESH,
        ).start()

    for target in (4, 7, 5, 6, 0, 1, 2, 3):
        needed = z < NZ - 1 if target >= GROUP else z < GROUP - 1

        @pl.when(jnp.logical_and(needed, z != target))
        def _():
            z_send_to(target)

    member = lax.rem(z, GROUP)
    z_in[z] = total[pl.ds(2 * pair(member), 2)]

    def z_wait(k):
        @pl.when(z != k)
        def _():
            moved(z_in.at[k], z_recv.at[k])

    def c_send_to(target):
        @pl.when(z != target)
        def _():
            pltpu.make_async_remote_copy(
                src_ref=carry.at[target], dst_ref=c_in.at[pl.ds(2 * pair(member), 2)], send_sem=c_send, recv_sem=c_recv.at[member],
                device_id=to(target * NX + x, s), device_id_type=MESH,
            ).start()

        @pl.when(z == target)
        def _():
            c_in[pl.ds(2 * pair(member), 2)] = carry[target]

    @pl.when(z < GROUP)
    def _():
        running = jnp.zeros((2, PIECE, D), F32)
        for k in range(GROUP - 1):
            z_wait(k)
            running = running + z_in[k].astype(F32)
            carry[k + 1] = running.astype(BF16)
            c_send_to(k + 1)

    @pl.when(z >= GROUP)
    def _():
        running = jnp.zeros((2, PIECE, D), F32)
        for k in range(NZ - 1):
            z_wait(k)
            running = running + z_in[k].astype(F32)
            if k + 1 >= GROUP:
                carry[k + 1] = running.astype(BF16)
                c_send_to(k + 1)

    pl.when(z > 0)(next_wait)
    forward()

    @pl.when(z == 0)
    def _():
        c_in[...] = jnp.zeros(c_in.shape, BF16)

    own_slot = lax.rem(own, 16)

    def u_send(x_to, frame):
        for core, out in enumerate((out_a, out_b)):

            @pl.when(lax.rem(s, 2) == core)
            def _():
                pltpu.make_async_remote_copy(
                    src_ref=done.at[x_to, frame], dst_ref=out.at[own_slot], send_sem=u_sent, recv_sem=u_recv,
                    device_id=to(z * NX + x_to, frame), device_id_type=MESH,
                ).start()

    def u_frames(j, kept):
        holder = lax.rem(member + j, GROUP)
        frames = pl.ds(2 * pair(holder), 2)

        @pl.when(jnp.logical_and(z > 0, j > 0))
        def _():
            moved(c_in.at[frames], c_recv.at[holder])

        carried = c_in[frames].astype(F32).reshape(2 * PIECE, D)
        for step in range(NX):
            rows = pl.ds(pl.multiple_of(pair(holder) * 2 * PIECE, 2 * PIECE), 2 * PIECE)
            carried = carried + drift[step, rows, :]
            done[step, frames] = carried.reshape(2, PIECE, D).astype(BF16)

        def u_start(k, held):
            x_to, frame = lax.rem(x + 2 + k // 2, NX), 2 * pair(holder) + lax.rem(s + 1 + k, 2)

            @pl.when(jnp.logical_or(x_to != x, frame != s))
            def _():
                u_send(x_to, frame)

            return held

        lax.fori_loop(0, 2 * NX, u_start, 0)
        return kept

    lax.fori_loop(0, GROUP, u_frames, 0)
    for core, out in enumerate((out_a, out_b)):

        @pl.when(lax.rem(s, 2) == core)
        def _():
            pltpu.make_async_copy(done.at[x, s], out.at[own_slot], own_sem).start()

    @pl.when(z < NZ - 1)
    def _():
        moved(state.at[NX], forward_recv)

    @pl.when(z == NZ - 1)
    def _():
        state[NX] = jnp.zeros(state.shape[1:], BF16)

    for step in range(NX):
        difference = done[step].astype(F32) - state[step + 1].astype(F32)
        squares = jnp.sum(difference * difference, axis=0)
        tile = squares[:, :128]
        for t in range(1, D // 128):
            tile = tile + squares[:, t * 128 : (t + 1) * 128]
        part[step] = jnp.sum(tile, axis=0, keepdims=True)

    def p_start(k, _):
        x_to, s_to = other(k, x, s)
        pltpu.make_async_remote_copy(
            src_ref=part.at[x_to], dst_ref=parts.at[x * NS + s], send_sem=p_send, recv_sem=p_recv,
            device_id=to(z * NX + x_to, s_to), device_id_type=MESH,
        ).start()
        return _

    lax.fori_loop(0, NX * NS - 1, p_start, 0)
    keep_part = pltpu.make_async_copy(part.at[x], parts.at[x * NS + s], own_part_sem)
    keep_part.start()

    moved(temper.at[pl.ds(0, NX - 1)], temper_send)
    moved(mine.at[pl.ds(0, NX * NS - 1)], y_send)

    moved(mine.at[pl.ds(0, NX * NS - 1)], next_send)

    @pl.when(z > 0)
    def _():
        moved(state.at[0], forward_send)


    @pl.when(z < GROUP - 1)
    def _():
        moved(z_in.at[pl.ds(0, 7)], z_send)

    @pl.when(z == GROUP - 1)
    def _():
        moved(z_in.at[pl.ds(0, 4)], z_send)

    @pl.when(jnp.logical_and(z >= GROUP, z < NZ - 1))
    def _():
        moved(z_in.at[pl.ds(0, 3)], z_send)

    few = jnp.logical_and(z > 0, z < GROUP)

    @pl.when(few)
    def _():
        moved(carry.at[pl.ds(0, 2)], c_send)

    @pl.when(jnp.logical_not(few))
    def _():
        moved(carry.at[pl.ds(0, 3)], c_send)

    moved(mine.at[0], own_sem)
    keep_part.wait()
    moved(mine.at[pl.ds(0, NX * NS - 1)], u_sent)
    moved(parts.at[pl.ds(0, NX * NS - 1)], p_send)
    moved(mine.at[pl.ds(0, NX * NS - 1)], u_recv)
    moved(parts.at[pl.ds(0, NX * NS - 1)], p_recv)


def finish(first_ref, second_ref, parts_ref, out, change_ref, sem):
    copies = [
        pltpu.make_async_copy(ref, out.at[pl.ds(i * 16, 16)], sem.at[i])
        for i, ref in enumerate((first_ref, second_ref))
    ]
    for copy in copies:
        copy.start()
    change_ref[0] = jnp.sum(jnp.sum(parts_ref[...], axis=0)) * (1.0 / (NS * ROWS * D))
    for copy in copies:
        copy.wait()


def body(latents, timesteps, step_sizes, modulation, spatial_qkv, spatial_out, temporal_qkv, temporal_out):
    dma = pltpu.SemaphoreType.DMA

    def vmem(*shape, dtype=BF16):
        return pltpu.VMEM(shape, dtype)

    def pieces(*count):
        return pltpu.VMEM((count or (NX * NS,)) + (PIECE, D), BF16)

    half_rows = jax.ShapeDtypeStruct((NX * NS // 2, PIECE, D), BF16)
    table = modulation.shape[0]
    first, second, parts = pl.pallas_call(
        kernel,
        out_shape=(half_rows, half_rows, jax.ShapeDtypeStruct((NX * NS, 1, 128), F32)),
        in_specs=[pl.BlockSpec(memory_space=pl.ANY)] * 8,
        out_specs=(pl.BlockSpec(memory_space=pl.ANY),) * 3,
        scratch_shapes=[
            pltpu.SMEM((1,), jnp.int32), pltpu.SMEM((1,), F32),
            pieces(), vmem(table, 6 * D),
            vmem(3 * E, D), vmem(E, D), vmem(3 * E, D), vmem(E, D),
            vmem(8, 6 * D, dtype=F32), vmem(ROWS, D),
            vmem(3 * E, ROWS, dtype=F32), vmem(2, ROWS, ROWS, dtype=F32), vmem(E, ROWS, dtype=F32),
            pieces(), pieces(), vmem(NX, 8, D, dtype=F32), pieces(NX + 1, NS),
            vmem(NX, STEP_ROWS, D, dtype=F32),
            pieces(NZ), pieces(NZ, 2), pieces(NZ, 2), pieces(NZ), pieces(NX, NS),
            vmem(NX, 1, 128, dtype=F32),
            dma((9,)), dma, dma, dma, dma, dma, dma, dma, dma,
            dma, dma((NZ,)), dma, dma((GROUP,)), dma, dma, dma, dma, dma, dma,
        ],
        compiler_params=pltpu.CompilerParams(
            collective_id=0, has_side_effects=True, vmem_limit_bytes=54374 * 1024
        ),
        cost_estimate=pl.CostEstimate(
            flops=2800000000, bytes_accessed=12000000, transcendentals=1000000
        ),
    )(
        latents.reshape(NX * NS, PIECE, D), timesteps, step_sizes, modulation,
        spatial_qkv.T, spatial_out, temporal_qkv.T, temporal_out,
    )
    updated, change = pl.pallas_call(
        finish,
        out_shape=(jax.ShapeDtypeStruct((NX * NS, PIECE, D), BF16), jax.ShapeDtypeStruct((1,), F32)),
        in_specs=[pl.BlockSpec(memory_space=pl.ANY)] * 2 + [pl.BlockSpec(memory_space=pltpu.VMEM)],
        out_specs=(pl.BlockSpec(memory_space=pl.ANY), pl.BlockSpec(memory_space=pltpu.SMEM)),
        scratch_shapes=[dma((2,))],
        compiler_params=pltpu.CompilerParams(vmem_limit_bytes=4 * 1024 * 1024),
    )(first, second, parts)
    return updated.reshape(latents.shape), change


def solution(mesh):
    in_specs = (P("step", "seq", None, None), P("step"), P("step"), P(), P(), P(), P(), P())
    out_specs = (P("step", "seq", None, None), P("step"))
    return jax.shard_map(body, mesh=mesh, in_specs=in_specs, out_specs=out_specs, check_vma=False)
```

```python
import math

import jax
import jax.numpy as jnp
from jax import lax
from jax.experimental import pallas as pl
from jax.experimental.pallas import tpu as pltpu
from jax.sharding import PartitionSpec as P

UNROLL = 7
PROJECT = 864
MESH = pl.DeviceIdType.MESH
F32 = jnp.float32
BF16 = jnp.bfloat16

D = 1152
HEADS = 8
HEAD_DIM = 72
E = HEADS * HEAD_DIM
ROWS = 256
HALF = 128
PIECE = 8
NX = 4
NZ = 8
NS = 8
GROUP = 4
STEP_ROWS = NS * PIECE
EPS = 1e-6
LOG2E = 1.4426950408889634
Q_SCALE = 3.0 / math.sqrt(HEAD_DIM) * LOG2E


NEAR_LAST = [
    (2, 2), (2, 1), (2, 3), (1, 2), (3, 2), (1, 1), (3, 3), (1, 3),
    (3, 1), (2, 0), (0, 2), (1, 0), (0, 1), (3, 0), (0, 3), (0, 0),
]
X_OFFSETS = sum(dx << (2 * j) for j, (dx, _) in enumerate(NEAR_LAST))
Y_OFFSETS = sum(dy << (2 * j) for j, (_, dy) in enumerate(NEAR_LAST))


def chip(j, x, y):
    dx = lax.rem(lax.shift_right_logical(jnp.int32(X_OFFSETS), 2 * j), 4)
    dy = lax.rem(lax.shift_right_logical(jnp.int32(Y_OFFSETS), 2 * j), 4)
    return lax.rem(x + dx, 4), lax.rem(y + dy, 4)


def other(j, x, s):
    x_to, y_to = chip(j // 2, x, s // 2)
    return x_to, y_to * 2 + lax.rem(s + 1 + lax.rem(j, 2), 2)


def layer_norm(values):
    center = values - jnp.mean(values, axis=-1, keepdims=True)
    spread = jnp.mean(center * center, axis=-1, keepdims=True)
    return center * lax.rsqrt(spread + EPS)


def attend(raw, heads, scores, blocks, mask):
    def unit(start, scale):
        values = raw[pl.ds(pl.multiple_of(start, 8), HEAD_DIM), :]
        squares = jnp.sum(values * values, axis=0, keepdims=True)
        return values * (lax.rsqrt(squares * (1.0 / HEAD_DIM) + EPS) * scale)

    def ask(head):
        asked = unit(head * HEAD_DIM, Q_SCALE).astype(BF16)
        keys = unit(E + head * HEAD_DIM, 1.0).T.astype(BF16)
        for at in blocks:
            scores[lax.rem(head, 2), at, : at.stop - at.start] = jnp.dot(
                keys[at, :], asked[:, at], preferred_element_type=F32
            )

    def answer(head):
        values = raw[pl.ds(pl.multiple_of(2 * E + head * HEAD_DIM, 8), HEAD_DIM), :].astype(BF16)
        for at in blocks:
            weights = jnp.exp2(scores[lax.rem(head, 2), at, : at.stop - at.start])
            if mask is not None:
                weights = jnp.where(mask, weights, 0.0)
            inverse = 1.0 / jnp.sum(weights, axis=0, keepdims=True)
            mixed = jnp.dot(values[:, at], weights.astype(BF16), preferred_element_type=F32)
            heads[pl.ds(pl.multiple_of(head * HEAD_DIM, 8), HEAD_DIM), at] = mixed * inverse

    def one_head(head, _):
        ask(head + 1)
        answer(head)
        return _

    ask(0)
    lax.fori_loop(0, HEADS - 1, one_head, 0, unroll=UNROLL)
    answer(HEADS - 1)


def kernel(
    lat_hbm, time_hbm, size_hbm, mod_hbm, w1_hbm, o1_hbm, w2_hbm, o2_hbm,
    out_a, out_b, parts,
    time_ref, size_ref, lat, mod, w1, o1, w2, o2, cond, inputs, raw, scores, heads,
    after, mine, temper, state, drift, total, z_in, carry, c_in, done, part,
    local_sem, temper_send, temper_recv, y_send, y_recv, next_send, next_recv, forward_send, forward_recv,
    z_send, z_recv, c_send, c_recv, u_sent, u_recv, p_send, p_recv, own_sem, own_part_sem,
):
    me = lax.axis_index("step")
    s = lax.axis_index("seq")
    z, x = me // NX, lax.rem(me, NX)

    loads = [
        pltpu.make_async_copy(src, dst, local_sem.at[i])
        for i, (src, dst) in enumerate(
            [
                (mod_hbm, mod), (lat_hbm, lat), (w1_hbm.at[pl.ds(0, PROJECT)], w1.at[pl.ds(0, PROJECT)]), (o1_hbm, o1), (w2_hbm, w2), (o2_hbm, o2),
                (time_hbm, time_ref), (size_hbm, size_ref),
                (w1_hbm.at[pl.ds(PROJECT, PROJECT)], w1.at[pl.ds(PROJECT, PROJECT)]),
            ]
        )
    ]
    for i in (6, 7, 0, 1, 2, 8, 3, 4, 5):
        loads[i].start()

    def to(step, seq):
        return {"step": step, "seq": seq}

    def greet(step, seq):
        pl.semaphore_signal(barrier, inc=1, device_id=to(step, seq), device_id_type=MESH)

    barrier = pltpu.get_barrier_semaphore()

    def greet_plane(k, _):
        greet(z * NX + lax.rem(x + k // NS, NX), lax.rem(s + lax.rem(k, NS), NS))
        return _

    lax.fori_loop(1, NX * NS, greet_plane, 0)

    def greet_planes(k, _):
        greet(lax.rem(z + k, NZ) * NX + x, s)
        return _

    lax.fori_loop(1, NZ, greet_planes, 0)

    loads[6].wait()
    loads[7].wait()
    loads[0].wait()
    one_hot = (lax.broadcasted_iota(jnp.int32, (16, mod.shape[0]), 1) == time_ref[0]).astype(BF16)
    cond[...] = jnp.dot(one_hot, mod[...], preferred_element_type=F32)[:8]

    def vector(i):
        return cond[0:1, i * D : (i + 1) * D]

    temper[x] = jnp.concatenate(
        [vector(3), 1.0 + vector(4), vector(5) * size_ref[0], jnp.broadcast_to(size_ref[0], (5, D))], axis=0
    )

    def moved(ref, sem):
        pltpu.make_async_copy(ref, ref, sem).wait()

    def normal_in(src, i, shift, scale, pieces):
        rows = pl.ds(pl.multiple_of(i * pieces * PIECE, pieces * PIECE), pieces * PIECE)
        values = src[pl.ds(i * pieces, pieces)].astype(F32).reshape(pieces * PIECE, D)
        inputs[rows, :] = (layer_norm(values) * scale + shift).astype(BF16)

    loads[1].wait()

    def spatial_in(i, _):
        normal_in(lat, i, vector(0), 1.0 + vector(1), 16)
        return _

    lax.fori_loop(0, 2, spatial_in, 0)

    contract_last = (((1,), (1,)), ((), ()))
    contract_first = (((0,), (0,)), ((), ()))

    def project(weights, i):
        rows = pl.ds(pl.multiple_of(i * PROJECT, 16), PROJECT)
        raw[rows, :] = lax.dot_general(
            weights[rows, :], inputs[...], contract_last, preferred_element_type=F32
        )

    def first_project(i, _):
        @pl.when(i == 0)
        def _():
            loads[2].wait()

        @pl.when(i == 1)
        def _():
            loads[8].wait()

        project(w1, i)
        return i

    lax.fori_loop(0, 3 * E // PROJECT, first_project, 0)
    attend(raw, heads, scores, (slice(0, ROWS),), None)
    loads[3].wait()

    pl.semaphore_wait(barrier, NX * NS - 1 + NZ - 1)

    def place(x_at, s_at):
        return lax.rem(s_at, 2) * 16 + (s_at // 2) * 4 + x_at

    own = place(x, s)

    def next_start(k, _):
        x_to, s_to = other(k, x, s)
        pltpu.make_async_remote_copy(
            src_ref=lat.at[place(x_to, s_to)], dst_ref=state.at[x, s], send_sem=next_send, recv_sem=next_recv,
            device_id=to(z * NX + x_to, s_to), device_id_type=MESH,
        ).start()
        return _

    def next_all():
        lax.fori_loop(0, NX * NS - 1, next_start, 0)
        state[x, s] = lat[own]

    def next_wait():
        moved(mine.at[pl.ds(0, NX * NS - 1)], next_recv)

    def forward():
        @pl.when(z > 0)
        def _():
            pltpu.make_async_remote_copy(
                src_ref=state.at[0], dst_ref=state.at[NX], send_sem=forward_send, recv_sem=forward_recv,
                device_id=to(me - NX, s), device_id_type=MESH,
            ).start()

    for k in range(1, NX):
        pltpu.make_async_remote_copy(
            src_ref=temper.at[x], dst_ref=temper.at[x], send_sem=temper_send, recv_sem=temper_recv,
            device_id=to(z * NX + lax.rem(x + k, NX), s), device_id_type=MESH,
        ).start()

    for half in range(2):
        rows = slice(half * HALF, (half + 1) * HALF)
        pieces = slice(half * 16, (half + 1) * 16)
        shown = lax.dot_general(
            heads[:, rows].astype(BF16), o1[...], contract_first, preferred_element_type=F32
        )
        latent = lat[pieces].astype(F32).reshape(HALF, D)
        after[pieces] = (latent + vector(2) * shown).reshape(16, PIECE, D).astype(BF16)

        def y_start(k, _):
            x_to, y_to = chip(k, x, s // 2)
            s_to = y_to * 2 + half

            @pl.when(jnp.logical_or(x_to != x, s_to != s))
            def _():
                pltpu.make_async_remote_copy(
                    src_ref=after.at[place(x_to, s_to)], dst_ref=mine.at[x * NS + s],
                    send_sem=y_send, recv_sem=y_recv,
                    device_id=to(z * NX + x_to, s_to), device_id_type=MESH,
                ).start()

            return k

        lax.fori_loop(0, 16, y_start, 0)
    mine[x * NS + s] = after[own]
    pl.when(z < GROUP)(next_all)

    loads[4].wait()
    loads[5].wait()
    moved(temper.at[pl.ds(0, NX - 1)], temper_recv)
    moved(mine.at[pl.ds(0, NX * NS - 1)], y_recv)
    pl.when(z >= GROUP)(next_all)

    def temporal_in(i, _):
        normal_in(mine, i, temper[i, 0:1, :], temper[i, 1:2, :], NS)
        return _

    lax.fori_loop(0, NX, temporal_in, 0, unroll=2)

    def second_project(i, _):
        project(w2, i)
        return _

    lax.fori_loop(0, 3 * E // PROJECT, second_project, 0)
    row = lax.broadcasted_iota(jnp.int32, (HALF, HALF), 0)
    col = lax.broadcasted_iota(jnp.int32, (HALF, HALF), 1)
    same = jnp.logical_and(row // STEP_ROWS == col // STEP_ROWS, lax.rem(row, PIECE) == lax.rem(col, PIECE))
    attend(raw, heads, scores, (slice(0, HALF), slice(HALF, ROWS)), same)
    for half in range(2):
        rows = slice(half * HALF, (half + 1) * HALF)
        shown = lax.dot_general(
            heads[:, rows].astype(BF16), o2[...], contract_first, preferred_element_type=F32
        )
        for i in range(2):
            step = half * 2 + i
            rows_in = mine[step * NS : (step + 1) * NS].astype(F32).reshape(STEP_ROWS, D)
            drift[step] = (
                rows_in * temper[step, 3:4, :]
                + temper[step, 2:3, :] * shown[i * STEP_ROWS : (i + 1) * STEP_ROWS]
            )

    @pl.when(z == 0)
    def _():
        next_wait()
        drift[0] = drift[0] + state[0].astype(F32).reshape(STEP_ROWS, D)

    everything = drift[0] + drift[1] + drift[2] + drift[3]
    total[...] = everything.reshape(NS, PIECE, D).astype(BF16)

    def pair(holder):
        return lax.rem(holder + x + s // 2, GROUP)

    def z_send_to(target):
        pltpu.make_async_remote_copy(
            src_ref=total.at[pl.ds(2 * pair(target % GROUP), 2)], dst_ref=z_in.at[z],
            send_sem=z_send, recv_sem=z_recv.at[z],
            device_id=to(target * NX + x, s), device_id_type=MESH,
        ).start()

    for target in (0, 3, 1, 2, 4, 7, 5, 6):
        needed = z < NZ - 1 if target >= GROUP else z < GROUP - 1

        @pl.when(jnp.logical_and(needed, z != target))
        def _():
            z_send_to(target)

    member = lax.rem(z, GROUP)
    z_in[z] = total[pl.ds(2 * pair(member), 2)]

    def z_wait(k):
        @pl.when(z != k)
        def _():
            moved(z_in.at[k], z_recv.at[k])

    def c_send_to(target):
        @pl.when(z != target)
        def _():
            pltpu.make_async_remote_copy(
                src_ref=carry.at[target], dst_ref=c_in.at[pl.ds(2 * pair(member), 2)], send_sem=c_send, recv_sem=c_recv.at[member],
                device_id=to(target * NX + x, s), device_id_type=MESH,
            ).start()

        @pl.when(z == target)
        def _():
            c_in[pl.ds(2 * pair(member), 2)] = carry[target]

    @pl.when(z < GROUP)
    def _():
        running = jnp.zeros((2, PIECE, D), F32)
        for k in range(GROUP - 1):
            z_wait(k)
            running = running + z_in[k].astype(F32)
            carry[k + 1] = running.astype(BF16)
            c_send_to(k + 1)

    @pl.when(z >= GROUP)
    def _():
        running = jnp.zeros((2, PIECE, D), F32)
        for k in range(NZ - 1):
            z_wait(k)
            running = running + z_in[k].astype(F32)
            if k + 1 >= GROUP:
                carry[k + 1] = running.astype(BF16)
                c_send_to(k + 1)

    pl.when(z > 0)(next_wait)
    forward()

    @pl.when(z == 0)
    def _():
        c_in[...] = jnp.zeros(c_in.shape, BF16)

    own_slot = lax.rem(own, 16)

    def u_send(x_to, frame):
        for core, out in enumerate((out_a, out_b)):

            @pl.when(lax.rem(s, 2) == core)
            def _():
                pltpu.make_async_remote_copy(
                    src_ref=done.at[x_to, frame], dst_ref=out.at[own_slot], send_sem=u_sent, recv_sem=u_recv,
                    device_id=to(z * NX + x_to, frame), device_id_type=MESH,
                ).start()

    def u_frames(j, kept):
        holder = lax.rem(member + j, GROUP)
        frames = pl.ds(2 * pair(holder), 2)

        @pl.when(jnp.logical_and(z > 0, j > 0))
        def _():
            moved(c_in.at[frames], c_recv.at[holder])

        carried = c_in[frames].astype(F32).reshape(2 * PIECE, D)
        for step in range(NX):
            rows = pl.ds(pl.multiple_of(pair(holder) * 2 * PIECE, 2 * PIECE), 2 * PIECE)
            carried = carried + drift[step, rows, :]
            done[step, frames] = carried.reshape(2, PIECE, D).astype(BF16)

        def u_start(k, held):
            x_to, frame = lax.rem(x + 2 + k // 2, NX), 2 * pair(holder) + lax.rem(s + 1 + k, 2)

            @pl.when(jnp.logical_or(x_to != x, frame != s))
            def _():
                u_send(x_to, frame)

            return held

        lax.fori_loop(0, 2 * NX, u_start, 0)
        return kept

    lax.fori_loop(0, GROUP, u_frames, 0)
    for core, out in enumerate((out_a, out_b)):

        @pl.when(lax.rem(s, 2) == core)
        def _():
            pltpu.make_async_copy(done.at[x, s], out.at[own_slot], own_sem).start()

    @pl.when(z < NZ - 1)
    def _():
        moved(state.at[NX], forward_recv)

    @pl.when(z == NZ - 1)
    def _():
        state[NX] = jnp.zeros(state.shape[1:], BF16)

    for step in range(NX):
        difference = done[step].astype(F32) - state[step + 1].astype(F32)
        squares = jnp.sum(difference * difference, axis=0)
        tile = squares[:, :128]
        for t in range(1, D // 128):
            tile = tile + squares[:, t * 128 : (t + 1) * 128]
        part[step] = jnp.sum(tile, axis=0, keepdims=True)

    def p_start(k, _):
        x_to, s_to = other(k, x, s)
        pltpu.make_async_remote_copy(
            src_ref=part.at[x_to], dst_ref=parts.at[x * NS + s], send_sem=p_send, recv_sem=p_recv,
            device_id=to(z * NX + x_to, s_to), device_id_type=MESH,
        ).start()
        return _

    lax.fori_loop(0, NX * NS - 1, p_start, 0)
    keep_part = pltpu.make_async_copy(part.at[x], parts.at[x * NS + s], own_part_sem)
    keep_part.start()

    moved(temper.at[pl.ds(0, NX - 1)], temper_send)
    moved(mine.at[pl.ds(0, NX * NS - 1)], y_send)

    moved(mine.at[pl.ds(0, NX * NS - 1)], next_send)

    @pl.when(z > 0)
    def _():
        moved(state.at[0], forward_send)


    @pl.when(z < GROUP - 1)
    def _():
        moved(z_in.at[pl.ds(0, 7)], z_send)

    @pl.when(z == GROUP - 1)
    def _():
        moved(z_in.at[pl.ds(0, 4)], z_send)

    @pl.when(jnp.logical_and(z >= GROUP, z < NZ - 1))
    def _():
        moved(z_in.at[pl.ds(0, 3)], z_send)

    few = jnp.logical_and(z > 0, z < GROUP)

    @pl.when(few)
    def _():
        moved(carry.at[pl.ds(0, 2)], c_send)

    @pl.when(jnp.logical_not(few))
    def _():
        moved(carry.at[pl.ds(0, 3)], c_send)

    moved(mine.at[0], own_sem)
    keep_part.wait()
    moved(mine.at[pl.ds(0, NX * NS - 1)], u_sent)
    moved(parts.at[pl.ds(0, NX * NS - 1)], p_send)
    moved(mine.at[pl.ds(0, NX * NS - 1)], u_recv)
    moved(parts.at[pl.ds(0, NX * NS - 1)], p_recv)


def finish(first_ref, second_ref, parts_ref, out, change_ref, sem):
    copies = [
        pltpu.make_async_copy(ref, out.at[pl.ds(i * 16, 16)], sem.at[i])
        for i, ref in enumerate((first_ref, second_ref))
    ]
    for copy in copies:
        copy.start()
    change_ref[0] = jnp.sum(jnp.sum(parts_ref[...], axis=0)) * (1.0 / (NS * ROWS * D))
    for copy in copies:
        copy.wait()


def body(latents, timesteps, step_sizes, modulation, spatial_qkv, spatial_out, temporal_qkv, temporal_out):
    dma = pltpu.SemaphoreType.DMA

    def vmem(*shape, dtype=BF16):
        return pltpu.VMEM(shape, dtype)

    def pieces(*count):
        return pltpu.VMEM((count or (NX * NS,)) + (PIECE, D), BF16)

    half_rows = jax.ShapeDtypeStruct((NX * NS // 2, PIECE, D), BF16)
    table = modulation.shape[0]
    first, second, parts = pl.pallas_call(
        kernel,
        out_shape=(half_rows, half_rows, jax.ShapeDtypeStruct((NX * NS, 1, 128), F32)),
        in_specs=[pl.BlockSpec(memory_space=pl.ANY)] * 8,
        out_specs=(pl.BlockSpec(memory_space=pl.ANY),) * 3,
        scratch_shapes=[
            pltpu.SMEM((1,), jnp.int32), pltpu.SMEM((1,), F32),
            pieces(), vmem(table, 6 * D),
            vmem(3 * E, D), vmem(E, D), vmem(3 * E, D), vmem(E, D),
            vmem(8, 6 * D, dtype=F32), vmem(ROWS, D),
            vmem(3 * E, ROWS, dtype=F32), vmem(2, ROWS, ROWS, dtype=F32), vmem(E, ROWS, dtype=F32),
            pieces(), pieces(), vmem(NX, 8, D, dtype=F32), pieces(NX + 1, NS),
            vmem(NX, STEP_ROWS, D, dtype=F32),
            pieces(NZ), pieces(NZ, 2), pieces(NZ, 2), pieces(NZ), pieces(NX, NS),
            vmem(NX, 1, 128, dtype=F32),
            dma((9,)), dma, dma, dma, dma, dma, dma, dma, dma,
            dma, dma((NZ,)), dma, dma((GROUP,)), dma, dma, dma, dma, dma, dma,
        ],
        compiler_params=pltpu.CompilerParams(
            collective_id=0, has_side_effects=True, vmem_limit_bytes=54374 * 1024
        ),
        cost_estimate=pl.CostEstimate(
            flops=2800000000, bytes_accessed=12000000, transcendentals=1000000
        ),
    )(
        latents.reshape(NX * NS, PIECE, D), timesteps, step_sizes, modulation,
        spatial_qkv.T, spatial_out, temporal_qkv.T, temporal_out,
    )
    updated, change = pl.pallas_call(
        finish,
        out_shape=(jax.ShapeDtypeStruct((NX * NS, PIECE, D), BF16), jax.ShapeDtypeStruct((1,), F32)),
        in_specs=[pl.BlockSpec(memory_space=pl.ANY)] * 2 + [pl.BlockSpec(memory_space=pltpu.VMEM)],
        out_specs=(pl.BlockSpec(memory_space=pl.ANY), pl.BlockSpec(memory_space=pltpu.SMEM)),
        scratch_shapes=[dma((2,))],
        compiler_params=pltpu.CompilerParams(vmem_limit_bytes=4 * 1024 * 1024),
    )(first, second, parts)
    return updated.reshape(latents.shape), change


def solution(mesh):
    in_specs = (P("step", "seq", None, None), P("step"), P("step"), P(), P(), P(), P(), P())
    out_specs = (P("step", "seq", None, None), P("step"))
    return jax.shard_map(body, mesh=mesh, in_specs=in_specs, out_specs=out_specs, check_vma=False)
```
